1024 devices in a mesh: gx: 4 (over z_lo), gy: 16 (over z_hi, x), gz: 16 (over y, core).
Axes of the slice: x: 4, y: 8, z: 16 (z_hi: 4, z_lo: 4; z = z_hi * 4 + z_lo), core: 2. Of those that a mesh axis runs over, the one named last changes fastest.
Arguments:
- checkpoint: float32 [19, 32, 128, 512], P(None, 'gz', 'gy', 'gx'), may hold values from -0.067 to 0.734, as said below
- porosity: float32 [32, 128, 512], P('gz', 'gy', 'gx'), may hold values from 0.02 to 0.9
- cell_kind: int32 [32, 128, 512], P('gz', 'gy', 'gx'), may hold values from 0 to 3
- objective_weight: float32 [32, 128, 512], P('gz', 'gy', 'gx'), may hold values from 0.5 to 45
Outputs:
- adjoint_populations: float32 [19, 32, 128, 512], P(None, 'gz', 'gy', 'gx')
- porosity_sensitivity: float32 [32, 128, 512], P('gz', 'gy', 'gx')
- objective: float32 [], replicated
The draws below stay inside these ranges and needn't reach their ends.
Inputs may be any that keep to these rules, and one draw needn't show every extreme that they name: `cell_kind`: 0 marks fluid, 1 wall, 2 inlet, 3 outlet cells. `checkpoint`: each population is its lattice weight times a factor between -0.2 and 2.2.
All inputs are finite; a program needn't handle non-finite values.
Results may differ from the reference program's by a relative error of at most 0.0003.
Values sent between devices are 32-bit elements; how exact they have to be, the bound alone decides.
No kernel may reach another device: no remote copies, remote signals or barrier semaphores. Data moves between devices by JAX's collectives and lax.ppermute only.
A program may use at most 32 MiB of HBM per device.

```python
import math
import jax
import jax.numpy as jnp
import numpy as np
from jax import lax

Q = 19
STEPS = 2
NX = 512
NY = 128
NZ = 32


draw_weights = np.array([1.0 / 3.0] + [1.0 / 18.0] * 6 + [1.0 / 36.0] * 12, dtype=np.float32)


def draw_checkpoint(key, part):
    key = jax.random.fold_in(key, 11)
    extent = (Q, NZ, NY, NX)
    jitter = jnp.clip(0.35 * jax.random.normal(key, extent, jnp.float32), -1.2, 1.2)
    weights = jnp.asarray(draw_weights, dtype=jnp.float32).reshape(Q, 1, 1, 1)
    return weights * (1.0 + jitter)


def draw_objective_weight(key, part):
    key = jax.random.fold_in(key, 23)
    depth_ramp = jnp.arange(NZ, dtype=jnp.float32).reshape(NZ, 1, 1) / NZ
    cross_ramp = jnp.arange(NY, dtype=jnp.float32).reshape(1, NY, 1) / NY
    growth = (1.0 + 2.0 * depth_ramp) * (1.0 + 2.0 * cross_ramp)
    spread = jnp.exp(jax.random.uniform(key, (NZ, NY, NX), jnp.float32, 0.0, 2.302585))
    return 0.5 * spread * growth


def touch_ends(values, rng, least, top_value):
    spot = [jax.random.randint(jax.random.fold_in(rng, axis), (), 0, length) for axis, length in enumerate(values.shape)]
    longest = values.shape.index(max(values.shape))
    beside = spot[:longest] + [(spot[longest] + 1) % values.shape[longest]] + spot[longest + 1:]
    return values.at[tuple(spot)].set(least).at[tuple(beside)].set(top_value)


def block_scale(key, shape, shards, low, top_value):
    loudness, own = 1.0, jax.random.fold_in(key, 6)
    for axis_at, blocks in shards:
        steps = jnp.exp(jax.random.uniform(jax.random.fold_in(own, axis_at), (blocks,), jnp.float32, low / len(shards), top_value / len(shards)))
        loudness = loudness * jnp.repeat(steps, shape[axis_at] // blocks).reshape([-1 if axis == axis_at else 1 for axis in range(len(shape))])
    return loudness


def setup_inputs(seed: int = 0) -> dict:
    keys = jax.random.split(jax.random.key(seed), 5)
    return {
        "checkpoint": draw_checkpoint(jax.random.fold_in(keys[4], 71), 0),
        "porosity": jnp.clip(jnp.exp(math.log(0.9) - 3.8066625 * jax.random.uniform(keys[1], (NZ, NY, NX), jnp.float32) ** block_scale(keys[1], (NZ, NY, NX), ((0, 16), (1, 16), (2, 4)), -0.2, 0.2)), 0.02, 0.9),
        "cell_kind": touch_ends(jax.random.randint(keys[2], (NZ, NY, NX), 0, 4), jax.random.fold_in(keys[2], 1), 0, 3).astype(jnp.int32),
        "objective_weight": draw_objective_weight(jax.random.fold_in(keys[4], 71), 0),
    }


lattice_dirs = np.array([[0, 0, 0], [1, 0, 0], [-1, 0, 0], [0, 1, 0], [0, -1, 0], [0, 0, 1], [0, 0, -1], [1, 1, 0], [-1, -1, 0], [1, -1, 0], [-1, 1, 0], [1, 0, 1], [-1, 0, -1], [1, 0, -1], [-1, 0, 1], [0, 1, 1], [0, -1, -1], [0, 1, -1], [0, -1, 1]], dtype=np.float32)
lattice_weights = np.array([1.0 / 3.0] + [1.0 / 18.0] * 6 + [1.0 / 36.0] * 12, dtype=np.float32)
relaxation = 1.25
inflow_vector = (0.08, 0.0, 0.03)

def collide(populations, porosity, cell_kind):
    directions = jnp.asarray(lattice_dirs, dtype=jnp.float32)
    ones_tail = (1,) * (populations.ndim - 1)
    weights = jnp.asarray(lattice_weights, dtype=jnp.float32).reshape((19,) + ones_tail)
    density = lax.optimization_barrier(jnp.sum(populations, axis=0))
    moment = jnp.tensordot(directions.T, populations, axes=1, precision=lax.Precision.HIGHEST)
    inflow = jnp.asarray(inflow_vector, dtype=jnp.float32).reshape((3,) + ones_tail)
    damped = jnp.where(cell_kind == 1, 0.0, (1.0 - porosity) * moment)
    damped = damped + jnp.where(cell_kind == 2, inflow, 0.0)
    target = jnp.where(cell_kind == 3, 1.0, density)
    project = jnp.tensordot(directions, damped, axes=1, precision=lax.Precision.HIGHEST)
    square = lax.optimization_barrier(jnp.sum(damped * damped, axis=0))
    balance = weights * (target + 3.0 * project + 4.5 * project * project - 1.5 * square)
    return populations + relaxation * (balance - populations)

def shift_planes(padded, extent, orient):
    planes = []
    for member in range(19):
        start_x = 1 - orient * int(lattice_dirs[member, 0])
        start_y = 1 - orient * int(lattice_dirs[member, 1])
        start_z = 1 - orient * int(lattice_dirs[member, 2])
        planes.append(padded[member, start_z:start_z + extent[0], start_y:start_y + extent[1], start_x:start_x + extent[2]])
    return jnp.stack(planes)

def stream(populations, orient):
    padded = jnp.pad(populations, ((0, 0), (1, 1), (1, 1), (1, 1)))
    return shift_planes(padded, populations.shape[1:], orient)

def collide_planes(populations, porosity, cell_kind):
    planar = jnp.moveaxis(populations, 1, 0)
    result = lax.map(lambda bundle: collide(bundle[0], bundle[1], bundle[2]), (planar, porosity, cell_kind))
    return jnp.moveaxis(result, 0, 1)

def adjoint_plane(bundle):
    values, carried, rates, kinds = bundle
    unused, pullback = jax.vjp(lambda inner, damping: collide(inner, damping, kinds), values, rates)
    return pullback(carried)

def reference(checkpoint, porosity, cell_kind, objective_weight):
    directions = jnp.asarray(lattice_dirs, dtype=jnp.float32)
    states = []
    populations = checkpoint
    for counter in range(STEPS):
        states.append(populations)
        populations = stream(collide_planes(populations, porosity, cell_kind), 1)
    moment = jnp.tensordot(directions.T, populations, axes=1, precision=lax.Precision.HIGHEST)
    summed = jnp.sum(0.5 * objective_weight * lax.optimization_barrier(jnp.sum(moment * moment, axis=0)))
    objective = summed / (NX * NY * NZ)
    adjoint = jnp.tensordot(directions, objective_weight * moment, axes=1, precision=lax.Precision.HIGHEST)
    sensitivity = jnp.zeros_like(porosity)
    for counter in reversed(range(STEPS)):
        carried = stream(adjoint, -1)
        planar, share = lax.map(adjoint_plane, (jnp.moveaxis(states[counter], 1, 0), jnp.moveaxis(carried, 1, 0), porosity, cell_kind))
        adjoint = jnp.moveaxis(planar, 0, 1)
        sensitivity = sensitivity + share
    return (adjoint, sensitivity, objective)
```

```python
import functools

import jax
import jax.numpy as jnp
import numpy as np
from jax import lax
from jax.experimental import pallas as pl
from jax.experimental.pallas import tpu as pltpu
from jax.sharding import PartitionSpec as P

DIRS = (
    (0, 0, 0),
    (1, 0, 0), (-1, 0, 0), (0, 1, 0), (0, -1, 0), (0, 0, 1), (0, 0, -1),
    (1, 1, 0), (-1, -1, 0), (1, -1, 0), (-1, 1, 0),
    (1, 0, 1), (-1, 0, -1), (1, 0, -1), (-1, 0, 1),
    (0, 1, 1), (0, -1, -1), (0, 1, -1), (0, -1, 1),
)
WEIGHTS = tuple(float(np.float32(w)) for w in [1.0 / 3.0] + [1.0 / 18.0] * 6 + [1.0 / 36.0] * 12)
PAIRS = tuple((i, i + 1) for i in range(1, 19, 2))
RELAX = 1.25
INFLOW = (0.08, 0.0, 0.03)

ZS, YS, XS = 2, 8, 128
HALO = 4
POR, KIND, WGT, FIELDS = 19, 20, 21, 22
SLOTS = XS // (2 * HALO)
EDGE_TILES = -(-FIELDS * ZS // SLOTS)

UP = tuple((c, 0) for c in range(19) if DIRS[c][2] == 1) + tuple(
    (c, 1) for c in range(19) if DIRS[c][2] >= 0
) + ((POR, 1), (KIND, 1))
DOWN = tuple((c, 1) for c in range(19) if DIRS[c][2] == -1) + tuple(
    (c, 0) for c in range(19) if DIRS[c][2] <= 0
) + ((POR, 0), (KIND, 0))
ZMSG = len(UP) + EDGE_TILES

VMEM_LIMIT = 48 * 1024 * 1024


def rot(value, shift, axis):
    shift = shift % value.shape[axis]
    return value if shift == 0 else pltpu.roll(value, shift, axis)


def lanes():
    return lax.broadcasted_iota(jnp.int32, (YS, XS), 1)


def low_rows():
    return lax.broadcasted_iota(jnp.int32, (YS, XS), 0) < HALO


def signed_sum(vector, parts):
    total = None
    for sign, part in zip(vector, parts):
        if sign == 0:
            continue
        if total is None:
            total = part if sign > 0 else -part
        else:
            total = total + part if sign > 0 else total - part
    return total


def momentum(get):
    parts = [None, None, None]
    for plus, minus in PAIRS:
        diff = get(plus) - get(minus)
        for axis in range(3):
            sign = DIRS[plus][axis]
            if sign:
                if parts[axis] is None:
                    parts[axis] = diff if sign > 0 else -diff
                else:
                    parts[axis] = parts[axis] + diff if sign > 0 else parts[axis] - diff
    return parts


def damping(kind, porosity):
    return jnp.where(kind == 2.0, 0.0, 1.0 - porosity)


def damped_of(moment, kind, scale):
    inlet = kind == 3.0
    return [
        scale * part + jnp.where(inlet, level, 0.0) if level else scale * part
        for part, level in zip(moment, INFLOW)
    ]


def post_collision(get, put, density, moment, kind, porosity, masked):
    damped = damped_of(moment, kind, damping(kind, porosity))
    target = jnp.where(kind == 4.0, 1.0, density)
    square = damped[0] * damped[0] + damped[1] * damped[1] + damped[2] * damped[2]
    base = RELAX * (target - 1.5 * square)
    keep = 1.0 - RELAX
    if masked:
        inside = kind > 0.5
        base = jnp.where(inside, base, 0.0)
        damped = [jnp.where(inside, part, 0.0) for part in damped]
        keep = jnp.where(inside, keep, 0.0)
    put(0, keep * get(0) + WEIGHTS[0] * base)
    for plus, minus in PAIRS:
        weight = WEIGHTS[plus]
        along = signed_sum(DIRS[plus], damped)
        even = weight * base + (4.5 * RELAX * weight) * (along * along)
        odd = (3.0 * RELAX * weight) * along
        put(plus, keep * get(plus) + (even + odd))
        put(minus, keep * get(minus) + (even - odd))


def adjoint_collision(get, put, moment, kind, porosity, masked):
    scale = damping(kind, porosity)
    damped = damped_of(moment, kind, scale)
    axis_even, axis_dot = None, [None, None, None]
    total = WEIGHTS[0] * get(0)
    slope = [None, None, None]
    for group in (PAIRS[:3], PAIRS[3:]):
        weight = WEIGHTS[group[0][0]]
        even_sum = None
        local = [None, None, None]
        for plus, minus in group:
            first, second = get(plus), get(minus)
            even, odd = first + second, first - second
            even_sum = even if even_sum is None else even_sum + even
            along = signed_sum(DIRS[plus], damped)
            term = odd + 3.0 * (along * even)
            for axis in range(3):
                sign = DIRS[plus][axis]
                if sign:
                    if local[axis] is None:
                        local[axis] = term if sign > 0 else -term
                    else:
                        local[axis] = local[axis] + term if sign > 0 else local[axis] - term
        total = total + weight * even_sum
        slope = [
            weight * new if old is None else old + weight * new for old, new in zip(slope, local)
        ]
    slope = [(3.0 * RELAX) * (part - total * drift) for part, drift in zip(slope, damped)]
    dot = slope[0] * moment[0] + slope[1] * moment[1] + slope[2] * moment[2]
    share = jnp.where(kind == 2.0, 0.0, -dot)
    even = jnp.where(kind == 4.0, 0.0, RELAX * total)
    back = [scale * part for part in slope]
    keep = 1.0 - RELAX
    if masked:
        inside = kind > 0.5
        even = jnp.where(inside, even, 0.0)
        back = [jnp.where(inside, part, 0.0) for part in back]
        keep = jnp.where(inside, keep, 0.0)
    put(0, keep * get(0) + even)
    for plus, minus in PAIRS:
        along = signed_sum(DIRS[plus], back)
        put(plus, keep * get(plus) + (even + along))
        put(minus, keep * get(minus) + (even - along))
    return share


def edges_kernel(f_ref, por_ref, kind_ref, wgt_ref, state_ref, edge_ref):
    for z in range(ZS):
        get = lambda i: f_ref[i, z]
        density = functools.reduce(lambda a, b: a + b, [get(i) for i in range(19)])
        kind = kind_ref[z].astype(jnp.float32) + 1.0

        def put(i, value):
            state_ref[i, z] = value

        post_collision(get, put, density, momentum(get), kind, por_ref[z], False)
        state_ref[POR, z] = por_ref[z]
        state_ref[KIND, z] = kind
        state_ref[WGT, z] = wgt_ref[z]
    slot_of = lanes() // (2 * HALO)
    for tile in range(EDGE_TILES):
        packed = jnp.zeros((YS, XS), jnp.float32)
        for slot in range(SLOTS):
            field, z = divmod(tile * SLOTS + slot, ZS)
            if field < FIELDS:
                moved = rot(state_ref[field, z], 2 * HALO * slot + HALO, 1)
                packed = jnp.where(slot_of == slot, moved, packed)
        edge_ref[tile] = packed


def rows_kernel(state_ref, left_ref, right_ref, edge_ref, low_ref, high_ref):
    from_left = lanes() % (2 * HALO) < HALO
    for tile in range(EDGE_TILES):
        edge_ref[tile] = jnp.where(from_left, left_ref[tile], right_ref[tile])
    low = low_rows()

    def pack(at, first, second):
        low_ref[at] = jnp.where(low, first, rot(second, HALO, 0))
        high_ref[at] = jnp.where(low, rot(first, HALO, 0), second)

    for field in range(FIELDS):
        pack(field, state_ref[field, 0], state_ref[field, 1])
    for at in range(0, EDGE_TILES, 2):
        second = edge_ref[min(at + 1, EDGE_TILES - 1)]
        pack(FIELDS + at // 2, edge_ref[at], second)


def planes_kernel(state_ref, edge_ref, below_ref, above_ref, wide_ref, side_ref, up_ref, down_ref):
    low = low_rows()

    def first(at):
        return jnp.where(low, above_ref[at], rot(below_ref[at], HALO, 0))

    def second(at):
        return jnp.where(low, rot(above_ref[at], HALO, 0), below_ref[at])

    for field in range(FIELDS):
        for z in range(ZS):
            wide_ref[field, z, 0] = state_ref[field, z]
        wide_ref[field, 0, 1] = first(field)
        wide_ref[field, 1, 1] = second(field)
    for tile in range(EDGE_TILES):
        side_ref[tile, 0] = edge_ref[tile]
        side_ref[tile, 1] = (second if tile % 2 else first)(FIELDS + tile // 2)
    for plan, ref in ((UP, up_ref), (DOWN, down_ref)):
        for at, (field, z) in enumerate(plan):
            ref[at] = wide_ref[field, z]
        for tile in range(EDGE_TILES):
            ref[len(plan) + tile] = side_ref[tile]


def join(main, packed, slot):
    main = main.reshape(2 * YS, XS)
    side = rot(packed.reshape(2 * YS, XS), XS - HALO - 2 * HALO * slot, 1)
    return jnp.concatenate([main, side], axis=1)


def forward_kernel(wide_ref, side_ref, lower_ref, upper_ref, aux_ref, flow_ref, part_ref, f_ref):
    def field_at(field, z):
        own = z % ZS
        tile, slot = divmod(field * ZS + own, SLOTS)
        if 0 <= z < ZS:
            return join(wide_ref[field, z], side_ref[tile], slot)
        plan, ref = (UP, lower_ref) if z < 0 else (DOWN, upper_ref)
        return join(ref[plan.index((field, own))], ref[len(plan) + tile], slot)

    for z in range(-1, ZS + 1):
        at = z + 1
        density = None
        moment = [None, None, None]
        for c in range(19):
            cx, cy, cz = DIRS[c]
            value = rot(rot(field_at(c, z - cz), cy, 0), cx, 1)
            f_ref[c, at] = value
            density = value if density is None else density + value
        get = lambda i: f_ref[i, at]
        moment = momentum(get)
        porosity, kind = field_at(POR, z), field_at(KIND, z)
        for axis in range(3):
            aux_ref[axis, at] = moment[axis]
        aux_ref[3, at] = porosity
        aux_ref[4, at] = kind

        def put(i, value):
            f_ref[i, at] = value

        post_collision(get, put, density, moment, kind, porosity, True)

    partial = jnp.zeros((YS, XS), jnp.float32)
    slot_of = lax.broadcasted_iota(jnp.int32, (2 * YS, XS), 1) // (2 * HALO)
    packed = jnp.zeros((2 * YS, XS), jnp.float32)
    for z in range(ZS):
        def arrived(i):
            cx, cy, cz = DIRS[i]
            return rot(rot(f_ref[i, z - cz + 1], cy, 0), cx, 1)

        moment = momentum(arrived)
        weight = field_at(WGT, z)
        for axis in range(3):
            flow = weight * moment[axis]
            partial = partial + flow[:YS, :XS] * moment[axis][:YS, :XS]
            slot = axis * ZS + z
            flow_ref[slot] = flow[:, :XS].reshape(2, YS, XS)
            moved = rot(flow[:, XS:], 2 * HALO * slot + HALO, 1)
            packed = jnp.where(slot_of == slot, moved, packed)
    flow_ref[3 * ZS] = packed.reshape(2, YS, XS)
    total = 0.5 * jnp.sum(partial, axis=0, keepdims=True)
    part_ref[...] = jnp.broadcast_to(total[None], part_ref.shape)


def backward_kernel(
    flow_ref, lower_ref, upper_ref, aux_ref, f_ref, por_ref, kind_ref, adjoint_ref, share_ref, g_ref
):
    def flow_at(axis, z):
        slot = axis * ZS + z % ZS
        ref = lower_ref if z < 0 else upper_ref if z >= ZS else flow_ref
        return join(ref[slot], ref[3 * ZS], slot)

    flows = [[flow_at(axis, z) for axis in range(3)] for z in range(-2, ZS + 2)]
    shares = []
    for z in range(-1, ZS + 1):
        at = z + 1
        g_ref[0, at] = jnp.zeros((2 * YS, 2 * XS), jnp.float32)
        for i in range(1, 19):
            cx, cy, cz = DIRS[i]
            seed = signed_sum(DIRS[i], flows[z + cz + 2])
            g_ref[i, at] = rot(rot(seed, -cy, 0), -cx, 1)
        get = lambda i: g_ref[i, at]

        def put(i, value):
            g_ref[i, at] = value

        moment = [aux_ref[axis, at] for axis in range(3)]
        share = adjoint_collision(get, put, moment, aux_ref[4, at], aux_ref[3, at], True)
        if 0 <= z < ZS:
            shares.append(share[:YS, :XS])
    for z in range(ZS):
        for i in range(19):
            cx, cy, cz = DIRS[i]
            value = rot(g_ref[i, z + cz + 1], -cy, 0)[:YS]
            adjoint_ref[i, z] = rot(value, -cx, 1)[:, :XS]
        carried = lambda i: adjoint_ref[i, z]

        def put_out(i, value):
            adjoint_ref[i, z] = value

        moment = momentum(lambda i: f_ref[i, z])
        kind = kind_ref[z].astype(jnp.float32) + 1.0
        share = adjoint_collision(carried, put_out, moment, kind, por_ref[z], False)
        share_ref[z] = shares[z] + share


def spread_kernel(in_ref, out_ref):
    out_ref[...] = jnp.broadcast_to(jnp.sum(in_ref[...], axis=0, keepdims=True), out_ref.shape)


def call(kernel, outs, scratch=()):
    shapes = tuple(jax.ShapeDtypeStruct(shape, jnp.float32) for shape in outs)
    return pl.pallas_call(
        kernel,
        out_shape=shapes if len(shapes) > 1 else shapes[0],
        scratch_shapes=[pltpu.VMEM(shape, jnp.float32) for shape in scratch],
        compiler_params=pltpu.CompilerParams(vmem_limit_bytes=VMEM_LIMIT),
    )


def swap(axis, to_next, to_previous):
    count = lax.axis_size(axis)
    forward = [(i, i + 1) for i in range(count - 1)]
    backward = [(i + 1, i) for i in range(count - 1)]
    return lax.ppermute(to_next, axis, forward), lax.ppermute(to_previous, axis, backward)


def per_device(checkpoint, porosity, cell_kind, objective_weight):
    state, edge = call(edges_kernel, [(FIELDS, ZS, YS, XS), (EDGE_TILES, YS, XS)])(
        checkpoint, porosity, cell_kind, objective_weight
    )
    left, right = swap("gx", edge, edge)
    rows = (FIELDS + (EDGE_TILES + 1) // 2, YS, XS)
    edge, low, high = call(rows_kernel, [(EDGE_TILES, YS, XS), rows, rows])(state, left, right)
    below, above = swap("gy", high, low)
    wide, side, up, down = call(
        planes_kernel,
        [(FIELDS, ZS, 2, YS, XS), (EDGE_TILES, 2, YS, XS), (ZMSG, 2, YS, XS), (ZMSG, 2, YS, XS)],
    )(state, edge, below, above)
    lower, upper = swap("gz", up, down)
    field = (ZS + 2, 2 * YS, 2 * XS)
    group = lax.axis_size("gz")
    aux, flow, part = call(
        forward_kernel,
        [(5,) + field, (3 * ZS + 1, 2, YS, XS), (group, 1, XS)],
        [(19,) + field],
    )(wide, side, lower, upper)
    flow_lower, flow_upper = swap("gz", flow, flow)
    part = lax.all_to_all(part, "gz", 0, 0, tiled=True)
    plane = lax.axis_size("gx") * lax.axis_size("gy")
    part = call(spread_kernel, [(plane, 1, XS)])(part)
    part = lax.all_to_all(part, ("gx", "gy"), 0, 0, tiled=True)
    cells = group * plane * ZS * YS * XS
    objective = jnp.sum(part) / cells
    adjoint, share = call(
        backward_kernel, [(19, ZS, YS, XS), (ZS, YS, XS)], [(19,) + field]
    )(flow, flow_lower, flow_upper, aux, checkpoint, porosity, cell_kind)
    return adjoint, share, objective


def solution(mesh):
    cells = P("gz", "gy", "gx")
    populations = P(None, "gz", "gy", "gx")
    return jax.shard_map(
        per_device,
        mesh=mesh,
        in_specs=(populations, cells, cells, cells),
        out_specs=(populations, cells, P()),
        check_vma=False,
    )
```

```python
import functools

import jax
import jax.numpy as jnp
import numpy as np
from jax import lax
from jax.experimental import pallas as pl
from jax.experimental.pallas import tpu as pltpu
from jax.sharding import PartitionSpec as P

DIRS = (
    (0, 0, 0),
    (1, 0, 0), (-1, 0, 0), (0, 1, 0), (0, -1, 0), (0, 0, 1), (0, 0, -1),
    (1, 1, 0), (-1, -1, 0), (1, -1, 0), (-1, 1, 0),
    (1, 0, 1), (-1, 0, -1), (1, 0, -1), (-1, 0, 1),
    (0, 1, 1), (0, -1, -1), (0, 1, -1), (0, -1, 1),
)
WEIGHTS = tuple(float(np.float32(w)) for w in [1.0 / 3.0] + [1.0 / 18.0] * 6 + [1.0 / 36.0] * 12)
PAIRS = tuple((i, i + 1) for i in range(1, 19, 2))
RELAX = 1.25
INFLOW = (0.08, 0.0, 0.03)

ZS, YS, XS = 2, 8, 128
HALO = 4
POR, KIND, WGT, FIELDS = 19, 20, 21, 22
SLOTS = XS // (2 * HALO)
EDGE_TILES = -(-FIELDS * ZS // SLOTS)

UP = tuple((c, 0) for c in range(19) if DIRS[c][2] == 1) + tuple(
    (c, 1) for c in range(19) if DIRS[c][2] >= 0
) + ((POR, 1), (KIND, 1))
DOWN = tuple((c, 1) for c in range(19) if DIRS[c][2] == -1) + tuple(
    (c, 0) for c in range(19) if DIRS[c][2] <= 0
) + ((POR, 0), (KIND, 0))
ZMSG = len(UP) + EDGE_TILES


def row_plan(sign, order):
    plan = []
    first = min(order[0], order[1])
    for field in range(FIELDS):
        for z in range(ZS):
            plan.append((field, z, first, 2))
    for z in range(ZS):
        for field in range(WGT):
            if field >= POR or DIRS[field][1] in (0, sign):
                plan.append((field, z, order[2], 1))
    for z in range(ZS):
        for field in range(19):
            if DIRS[field][1] == sign:
                plan.append((field, z, order[3], 1))
    return tuple(plan)


ROWS_LOW = row_plan(-1, (0, 1, 2, 3))
ROWS_HIGH = row_plan(1, (7, 6, 5, 4))
ROWS_MAIN = sum(rows for _, _, _, rows in ROWS_LOW)
ROWS_MSG = -(-(ROWS_MAIN + HALO * EDGE_TILES) // 8) * 8

VMEM_LIMIT = 48 * 1024 * 1024


def rot(value, shift, axis):
    shift = shift % value.shape[axis]
    return value if shift == 0 else pltpu.roll(value, shift, axis)


def lanes():
    return lax.broadcasted_iota(jnp.int32, (YS, XS), 1)


def signed_sum(vector, parts):
    total = None
    for sign, part in zip(vector, parts):
        if sign == 0:
            continue
        if total is None:
            total = part if sign > 0 else -part
        else:
            total = total + part if sign > 0 else total - part
    return total


def momentum(get):
    parts = [None, None, None]
    for plus, minus in PAIRS:
        diff = get(plus) - get(minus)
        for axis in range(3):
            sign = DIRS[plus][axis]
            if sign:
                if parts[axis] is None:
                    parts[axis] = diff if sign > 0 else -diff
                else:
                    parts[axis] = parts[axis] + diff if sign > 0 else parts[axis] - diff
    return parts


def damping(kind, porosity):
    return jnp.where(kind == 2.0, 0.0, 1.0 - porosity)


def damped_of(moment, kind, scale):
    inlet = kind == 3.0
    return [
        scale * part + jnp.where(inlet, level, 0.0) if level else scale * part
        for part, level in zip(moment, INFLOW)
    ]


def post_collision(get, put, density, moment, kind, porosity, masked):
    damped = damped_of(moment, kind, damping(kind, porosity))
    target = jnp.where(kind == 4.0, 1.0, density)
    square = damped[0] * damped[0] + damped[1] * damped[1] + damped[2] * damped[2]
    base = RELAX * (target - 1.5 * square)
    keep = 1.0 - RELAX
    if masked:
        inside = kind > 0.5
        base = jnp.where(inside, base, 0.0)
        damped = [jnp.where(inside, part, 0.0) for part in damped]
        keep = jnp.where(inside, keep, 0.0)
    put(0, keep * get(0) + WEIGHTS[0] * base)
    for plus, minus in PAIRS:
        weight = WEIGHTS[plus]
        along = signed_sum(DIRS[plus], damped)
        even = weight * base + (4.5 * RELAX * weight) * (along * along)
        odd = (3.0 * RELAX * weight) * along
        put(plus, keep * get(plus) + (even + odd))
        put(minus, keep * get(minus) + (even - odd))


def adjoint_collision(get, put, moment, kind, porosity, masked):
    scale = damping(kind, porosity)
    damped = damped_of(moment, kind, scale)
    axis_even, axis_dot = None, [None, None, None]
    total = WEIGHTS[0] * get(0)
    slope = [None, None, None]
    for group in (PAIRS[:3], PAIRS[3:]):
        weight = WEIGHTS[group[0][0]]
        even_sum = None
        local = [None, None, None]
        for plus, minus in group:
            first, second = get(plus), get(minus)
            even, odd = first + second, first - second
            even_sum = even if even_sum is None else even_sum + even
            along = signed_sum(DIRS[plus], damped)
            term = odd + 3.0 * (along * even)
            for axis in range(3):
                sign = DIRS[plus][axis]
                if sign:
                    if local[axis] is None:
                        local[axis] = term if sign > 0 else -term
                    else:
                        local[axis] = local[axis] + term if sign > 0 else local[axis] - term
        total = total + weight * even_sum
        slope = [
            weight * new if old is None else old + weight * new for old, new in zip(slope, local)
        ]
    slope = [(3.0 * RELAX) * (part - total * drift) for part, drift in zip(slope, damped)]
    dot = slope[0] * moment[0] + slope[1] * moment[1] + slope[2] * moment[2]
    share = jnp.where(kind == 2.0, 0.0, -dot)
    even = jnp.where(kind == 4.0, 0.0, RELAX * total)
    back = [scale * part for part in slope]
    keep = 1.0 - RELAX
    if masked:
        inside = kind > 0.5
        even = jnp.where(inside, even, 0.0)
        back = [jnp.where(inside, part, 0.0) for part in back]
        keep = jnp.where(inside, keep, 0.0)
    put(0, keep * get(0) + even)
    for plus, minus in PAIRS:
        along = signed_sum(DIRS[plus], back)
        put(plus, keep * get(plus) + (even + along))
        put(minus, keep * get(minus) + (even - along))
    return share


def parity(axis):
    return lax.axis_index(axis) % 2 == 1


def edges_kernel(f_hbm, por_hbm, kind_hbm, wgt_hbm, state_ref, edge_ref, f_ref, por_ref, kind_ref, wgt_ref, sems):
    copies = [
        pltpu.make_async_copy(source, target, sems.at[at])
        for at, (source, target) in enumerate(
            ((f_hbm, f_ref), (por_hbm, por_ref), (kind_hbm, kind_ref), (wgt_hbm, wgt_ref))
        )
    ]
    for copy in copies:
        copy.start()
    for copy in copies:
        copy.wait()
    for z in range(ZS):
        get = lambda i: f_ref[i, z]
        density = functools.reduce(lambda a, b: a + b, [get(i) for i in range(19)])
        kind = kind_ref[z].astype(jnp.float32) + 1.0

        def put(i, value):
            state_ref[i, z] = value

        post_collision(get, put, density, momentum(get), kind, por_ref[z], False)
        state_ref[POR, z] = por_ref[z]
        state_ref[KIND, z] = kind
        state_ref[WGT, z] = wgt_ref[z]
    slot_of = lanes() // (2 * HALO)
    for tile in range(EDGE_TILES):
        packed = jnp.zeros((YS, XS), jnp.float32)
        for slot in range(SLOTS):
            field, z = divmod(tile * SLOTS + slot, ZS)
            if field < FIELDS:
                moved = rot(state_ref[field, z], 2 * HALO * slot + HALO, 1)
                packed = jnp.where(slot_of == slot, moved, packed)
        edge_ref[tile] = packed


def rows_kernel(state_ref, odd_ref, even_ref, edge_ref, to_odd_ref, to_even_ref):
    from_left = (lanes() % (2 * HALO) < HALO).astype(jnp.int32)
    mine = (lax.axis_index("gx") % 2).astype(jnp.int32)
    for tile in range(EDGE_TILES):
        edge_ref[tile] = jnp.where(from_left == mine, even_ref[tile], odd_ref[tile])

    def pack(plan, start, ref):
        at = 0
        for field, z, row, rows in plan:
            ref[at : at + rows] = state_ref[field, z, row : row + rows]
            at += rows
        for tile in range(EDGE_TILES):
            at = ROWS_MAIN + HALO * tile
            ref[at : at + HALO] = edge_ref[tile, start : start + HALO]

    odd = parity("gy")

    @pl.when(odd)
    def _():
        pack(ROWS_LOW, 0, to_even_ref)
        pack(ROWS_HIGH, HALO, to_odd_ref)

    @pl.when(jnp.logical_not(odd))
    def _():
        pack(ROWS_HIGH, HALO, to_even_ref)
        pack(ROWS_LOW, 0, to_odd_ref)


def planes_kernel(state_ref, edge_ref, odd_ref, even_ref, wide_ref, side_ref, to_odd_ref, to_even_ref):
    for field in range(FIELDS):
        for z in range(ZS):
            wide_ref[field, z, 0] = state_ref[field, z]
    for tile in range(EDGE_TILES):
        side_ref[tile, 0] = edge_ref[tile]

    def unpack(plan, start, ref):
        at = 0
        for field, z, row, rows in plan:
            wide_ref[field, z, 1, row : row + rows] = ref[at : at + rows]
            at += rows
        for tile in range(EDGE_TILES):
            at = ROWS_MAIN + HALO * tile
            side_ref[tile, 1, start : start + HALO] = ref[at : at + HALO]

    odd = parity("gy")

    @pl.when(odd)
    def _():
        unpack(ROWS_HIGH, HALO, even_ref)
        unpack(ROWS_LOW, 0, odd_ref)

    @pl.when(jnp.logical_not(odd))
    def _():
        unpack(ROWS_LOW, 0, even_ref)
        unpack(ROWS_HIGH, HALO, odd_ref)

    def pack(plan, ref):
        for at, (field, z) in enumerate(plan):
            ref[at] = wide_ref[field, z]
        for tile in range(EDGE_TILES):
            ref[len(plan) + tile] = side_ref[tile]

    odd_z = parity("gz")

    @pl.when(odd_z)
    def _():
        pack(DOWN, to_even_ref)
        pack(UP, to_odd_ref)

    @pl.when(jnp.logical_not(odd_z))
    def _():
        pack(UP, to_even_ref)
        pack(DOWN, to_odd_ref)


def join(main, packed, slot):
    main = main.reshape(2 * YS, XS)
    side = rot(packed.reshape(2 * YS, XS), XS - HALO - 2 * HALO * slot, 1)
    return jnp.concatenate([main, side], axis=1)


def forward_kernel(wide_ref, side_ref, odd_ref, even_ref, aux_ref, flow_ref, part_ref, f_ref):
    odd = parity("gz")

    def field_at(field, z):
        own = z % ZS
        tile, slot = divmod(field * ZS + own, SLOTS)
        if 0 <= z < ZS:
            return join(wide_ref[field, z], side_ref[tile], slot)
        plan = UP if z < 0 else DOWN
        main, side = plan.index((field, own)), len(plan) + tile
        first, second = (even_ref, odd_ref) if z < 0 else (odd_ref, even_ref)
        return join(
            jnp.where(odd, first[main], second[main]),
            jnp.where(odd, first[side], second[side]),
            slot,
        )

    for z in range(-1, ZS + 1):
        at = z + 1
        density = None
        moment = [None, None, None]
        for c in range(19):
            cx, cy, cz = DIRS[c]
            value = rot(rot(field_at(c, z - cz), cy, 0), cx, 1)
            f_ref[c, at] = value
            density = value if density is None else density + value
        get = lambda i: f_ref[i, at]
        moment = momentum(get)
        porosity, kind = field_at(POR, z), field_at(KIND, z)
        for axis in range(3):
            aux_ref[axis, at] = moment[axis]
        aux_ref[3, at] = porosity
        aux_ref[4, at] = kind

        def put(i, value):
            f_ref[i, at] = value

        post_collision(get, put, density, moment, kind, porosity, True)

    partial = jnp.zeros((YS, XS), jnp.float32)
    slot_of = lax.broadcasted_iota(jnp.int32, (2 * YS, XS), 1) // (2 * HALO)
    packed = jnp.zeros((2 * YS, XS), jnp.float32)
    for z in range(ZS):
        def arrived(i):
            cx, cy, cz = DIRS[i]
            return rot(rot(f_ref[i, z - cz + 1], cy, 0), cx, 1)

        moment = momentum(arrived)
        weight = field_at(WGT, z)
        for axis in range(3):
            flow = weight * moment[axis]
            partial = partial + flow[:YS, :XS] * moment[axis][:YS, :XS]
            slot = axis * ZS + z
            flow_ref[slot] = flow[:, :XS].reshape(2, YS, XS)
            moved = rot(flow[:, XS:], 2 * HALO * slot + HALO, 1)
            packed = jnp.where(slot_of == slot, moved, packed)
    flow_ref[3 * ZS] = packed.reshape(2, YS, XS)
    total = 0.5 * jnp.sum(partial, axis=0, keepdims=True)
    part_ref[...] = jnp.broadcast_to(total[None], part_ref.shape)


def backward_kernel(
    flow_ref, odd_ref, even_ref, aux_ref, f_ref, por_ref, kind_ref, adjoint_ref, share_ref, g_ref
):
    odd = parity("gz")

    def flow_at(axis, z):
        slot = axis * ZS + z % ZS
        if 0 <= z < ZS:
            return join(flow_ref[slot], flow_ref[3 * ZS], slot)
        first, second = (even_ref, odd_ref) if z < 0 else (odd_ref, even_ref)
        return join(
            jnp.where(odd, first[slot], second[slot]),
            jnp.where(odd, first[3 * ZS], second[3 * ZS]),
            slot,
        )

    flows = [[flow_at(axis, z) for axis in range(3)] for z in range(-2, ZS + 2)]
    shares = []
    for z in range(-1, ZS + 1):
        at = z + 1
        g_ref[0, at] = jnp.zeros((2 * YS, 2 * XS), jnp.float32)
        for i in range(1, 19):
            cx, cy, cz = DIRS[i]
            seed = signed_sum(DIRS[i], flows[z + cz + 2])
            g_ref[i, at] = rot(rot(seed, -cy, 0), -cx, 1)
        get = lambda i: g_ref[i, at]

        def put(i, value):
            g_ref[i, at] = value

        moment = [aux_ref[axis, at] for axis in range(3)]
        share = adjoint_collision(get, put, moment, aux_ref[4, at], aux_ref[3, at], True)
        if 0 <= z < ZS:
            shares.append(share[:YS, :XS])
    for z in range(ZS):
        for i in range(19):
            cx, cy, cz = DIRS[i]
            value = rot(g_ref[i, z + cz + 1], -cy, 0)[:YS]
            adjoint_ref[i, z] = rot(value, -cx, 1)[:, :XS]
        carried = lambda i: adjoint_ref[i, z]

        def put_out(i, value):
            adjoint_ref[i, z] = value

        moment = momentum(lambda i: f_ref[i, z])
        kind = kind_ref[z].astype(jnp.float32) + 1.0
        share = adjoint_collision(carried, put_out, moment, kind, por_ref[z], False)
        share_ref[z] = shares[z] + share


def spread_kernel(in_ref, out_ref):
    out_ref[...] = jnp.broadcast_to(jnp.sum(in_ref[...], axis=0, keepdims=True), out_ref.shape)


def call(kernel, outs, scratch=(), **options):
    shapes = tuple(jax.ShapeDtypeStruct(shape, jnp.float32) for shape in outs)
    return pl.pallas_call(
        kernel,
        out_shape=shapes if len(shapes) > 1 else shapes[0],
        scratch_shapes=[
            pltpu.VMEM(shape, jnp.float32) if isinstance(shape, tuple) else shape for shape in scratch
        ],
        compiler_params=pltpu.CompilerParams(vmem_limit_bytes=VMEM_LIMIT),
        **options,
    )


def swap(axis, to_even, to_odd):
    count = lax.axis_size(axis)

    def partners(first):
        return [
            pair for low in range(first, count - 1, 2) for pair in ((low, low + 1), (low + 1, low))
        ]

    odd = lax.ppermute(to_odd, axis, partners(1))
    even = lax.ppermute(to_even, axis, partners(0))
    return odd, even


def per_device(checkpoint, porosity, cell_kind, objective_weight):
    brick = (ZS, YS, XS)
    state, edge = call(
        edges_kernel,
        [(FIELDS,) + brick, (EDGE_TILES, YS, XS)],
        [(19,) + brick, brick, pltpu.VMEM(brick, jnp.int32), brick, pltpu.SemaphoreType.DMA((4,))],
        in_specs=[pl.BlockSpec(memory_space=pl.ANY)] * 4,
    )(
        *(
            pltpu.with_memory_space_constraint(value, pltpu.HBM)
            for value in (checkpoint, porosity, cell_kind, objective_weight)
        )
    )
    rows = (ROWS_MSG, XS)
    edge, to_odd, to_even = call(rows_kernel, [(EDGE_TILES, YS, XS), rows, rows])(
        state, *swap("gx", edge, edge)
    )
    planes = (ZMSG, 2, YS, XS)
    wide, side, to_odd, to_even = call(
        planes_kernel, [(FIELDS, ZS, 2, YS, XS), (EDGE_TILES, 2, YS, XS), planes, planes]
    )(state, edge, *swap("gy", to_even, to_odd))
    field = (ZS + 2, 2 * YS, 2 * XS)
    group = lax.axis_size("gz")
    aux, flow, part = call(
        forward_kernel,
        [(5,) + field, (3 * ZS + 1, 2, YS, XS), (group, 1, XS)],
        [(19,) + field],
    )(wide, side, *swap("gz", to_even, to_odd))
    flow_odd, flow_even = swap("gz", flow, flow)
    part = lax.all_to_all(part, "gz", 0, 0, tiled=True)
    plane = lax.axis_size("gx") * lax.axis_size("gy")
    part = call(spread_kernel, [(plane, 1, XS)])(part)
    part = lax.all_to_all(part, ("gx", "gy"), 0, 0, tiled=True)
    cells = group * plane * ZS * YS * XS
    objective = jnp.sum(part) / cells
    adjoint, share = call(backward_kernel, [(19,) + brick, brick], [(19,) + field])(
        flow, flow_odd, flow_even, aux, checkpoint, porosity, cell_kind
    )
    return adjoint, share, objective


def solution(mesh):
    cells = P("gz", "gy", "gx")
    populations = P(None, "gz", "gy", "gx")
    return jax.shard_map(
        per_device,
        mesh=mesh,
        in_specs=(populations, cells, cells, cells),
        out_specs=(populations, cells, P()),
        check_vma=False,
    )
```

```python
import functools

import jax
import jax.numpy as jnp
import numpy as np
from jax import lax
from jax.experimental import pallas as pl
from jax.experimental.pallas import tpu as pltpu
from jax.sharding import PartitionSpec as P

DIRS = (
    (0, 0, 0),
    (1, 0, 0), (-1, 0, 0), (0, 1, 0), (0, -1, 0), (0, 0, 1), (0, 0, -1),
    (1, 1, 0), (-1, -1, 0), (1, -1, 0), (-1, 1, 0),
    (1, 0, 1), (-1, 0, -1), (1, 0, -1), (-1, 0, 1),
    (0, 1, 1), (0, -1, -1), (0, 1, -1), (0, -1, 1),
)
WEIGHTS = tuple(float(np.float32(w)) for w in [1.0 / 3.0] + [1.0 / 18.0] * 6 + [1.0 / 36.0] * 12)
PAIRS = tuple((i, i + 1) for i in range(1, 19, 2))
RELAX = 1.25
INFLOW = (0.08, 0.0, 0.03)

ZS, YS, XS = 2, 8, 128
HALO = 4
POR, KIND, WGT, FIELDS = 19, 20, 21, 22
SLOTS = XS // (2 * HALO)
EDGE_TILES = -(-FIELDS * ZS // SLOTS)

UP = tuple((c, 0) for c in range(19) if DIRS[c][2] == 1) + tuple(
    (c, 1) for c in range(19) if DIRS[c][2] >= 0
) + ((POR, 1), (KIND, 1))
DOWN = tuple((c, 1) for c in range(19) if DIRS[c][2] == -1) + tuple(
    (c, 0) for c in range(19) if DIRS[c][2] <= 0
) + ((POR, 0), (KIND, 0))
ZMSG = len(UP) + EDGE_TILES


def row_plan(sign, order):
    plan = []
    first = min(order[0], order[1])
    for field in range(FIELDS):
        for z in range(ZS):
            plan.append((field, z, first, 2))
    for z in range(ZS):
        for field in range(WGT):
            if field >= POR or DIRS[field][1] in (0, sign):
                plan.append((field, z, order[2], 1))
    for z in range(ZS):
        for field in range(19):
            if DIRS[field][1] == sign:
                plan.append((field, z, order[3], 1))
    return tuple(plan)


ROWS_LOW = row_plan(-1, (0, 1, 2, 3))
ROWS_HIGH = row_plan(1, (7, 6, 5, 4))
ROWS_MAIN = sum(rows for _, _, _, rows in ROWS_LOW)
ROWS_MSG = -(-(ROWS_MAIN + HALO * EDGE_TILES) // 8) * 8

VMEM_LIMIT = 48 * 1024 * 1024


def rot(value, shift, axis):
    shift = shift % value.shape[axis]
    return value if shift == 0 else pltpu.roll(value, shift, axis)


def lanes():
    return lax.broadcasted_iota(jnp.int32, (YS, XS), 1)


def signed_sum(vector, parts):
    total = None
    for sign, part in zip(vector, parts):
        if sign == 0:
            continue
        if total is None:
            total = part if sign > 0 else -part
        else:
            total = total + part if sign > 0 else total - part
    return total


def momentum(get):
    parts = [None, None, None]
    for plus, minus in PAIRS:
        diff = get(plus) - get(minus)
        for axis in range(3):
            sign = DIRS[plus][axis]
            if sign:
                if parts[axis] is None:
                    parts[axis] = diff if sign > 0 else -diff
                else:
                    parts[axis] = parts[axis] + diff if sign > 0 else parts[axis] - diff
    return parts


def damping(kind, porosity):
    return jnp.where(kind == 2.0, 0.0, 1.0 - porosity)


def damped_of(moment, kind, scale):
    inlet = kind == 3.0
    return [
        scale * part + jnp.where(inlet, level, 0.0) if level else scale * part
        for part, level in zip(moment, INFLOW)
    ]


def post_collision(get, put, density, moment, kind, porosity, masked, wanted=range(19)):
    damped = damped_of(moment, kind, damping(kind, porosity))
    target = jnp.where(kind == 4.0, 1.0, density)
    square = damped[0] * damped[0] + damped[1] * damped[1] + damped[2] * damped[2]
    base = RELAX * (target - 1.5 * square)
    keep = 1.0 - RELAX
    if masked:
        inside = kind > 0.5
        base = jnp.where(inside, base, 0.0)
        damped = [jnp.where(inside, part, 0.0) for part in damped]
        keep = jnp.where(inside, keep, 0.0)
    if 0 in wanted:
        put(0, keep * get(0) + WEIGHTS[0] * base)
    for plus, minus in PAIRS:
        if plus not in wanted and minus not in wanted:
            continue
        weight = WEIGHTS[plus]
        along = signed_sum(DIRS[plus], damped)
        even = weight * base + (4.5 * RELAX * weight) * (along * along)
        odd = (3.0 * RELAX * weight) * along
        if plus in wanted:
            put(plus, keep * get(plus) + (even + odd))
        if minus in wanted:
            put(minus, keep * get(minus) + (even - odd))


def adjoint_collision(get, put, moment, kind, porosity, masked, wanted=range(19)):
    scale = damping(kind, porosity)
    damped = damped_of(moment, kind, scale)
    total = WEIGHTS[0] * get(0)
    slope = [None, None, None]
    for group in (PAIRS[:3], PAIRS[3:]):
        weight = WEIGHTS[group[0][0]]
        even_sum = None
        local = [None, None, None]
        for plus, minus in group:
            first, second = get(plus), get(minus)
            even, odd = first + second, first - second
            even_sum = even if even_sum is None else even_sum + even
            along = signed_sum(DIRS[plus], damped)
            term = odd + 3.0 * (along * even)
            for axis in range(3):
                sign = DIRS[plus][axis]
                if sign:
                    if local[axis] is None:
                        local[axis] = term if sign > 0 else -term
                    else:
                        local[axis] = local[axis] + term if sign > 0 else local[axis] - term
        total = total + weight * even_sum
        slope = [
            weight * new if old is None else old + weight * new for old, new in zip(slope, local)
        ]
    slope = [(3.0 * RELAX) * (part - total * drift) for part, drift in zip(slope, damped)]
    dot = slope[0] * moment[0] + slope[1] * moment[1] + slope[2] * moment[2]
    share = jnp.where(kind == 2.0, 0.0, -dot)
    even = jnp.where(kind == 4.0, 0.0, RELAX * total)
    back = [scale * part for part in slope]
    keep = 1.0 - RELAX
    if masked:
        inside = kind > 0.5
        even = jnp.where(inside, even, 0.0)
        back = [jnp.where(inside, part, 0.0) for part in back]
        keep = jnp.where(inside, keep, 0.0)
    if 0 in wanted:
        put(0, keep * get(0) + even)
    for plus, minus in PAIRS:
        if plus not in wanted and minus not in wanted:
            continue
        along = signed_sum(DIRS[plus], back)
        if plus in wanted:
            put(plus, keep * get(plus) + (even + along))
        if minus in wanted:
            put(minus, keep * get(minus) + (even - along))
    return share


def parity(axis):
    return lax.axis_index(axis) % 2 == 1


def edges_kernel(f_hbm, por_hbm, kind_hbm, wgt_hbm, state_ref, edge_ref, f_ref, por_ref, kind_ref, wgt_ref, sems):
    copies = [
        pltpu.make_async_copy(source, target, sems.at[at])
        for at, (source, target) in enumerate(
            ((f_hbm, f_ref), (por_hbm, por_ref), (kind_hbm, kind_ref), (wgt_hbm, wgt_ref))
        )
    ]
    for copy in copies:
        copy.start()
    for copy in copies:
        copy.wait()
    for z in range(ZS):
        get = lambda i: f_ref[i, z]
        density = functools.reduce(lambda a, b: a + b, [get(i) for i in range(19)])
        kind = kind_ref[z].astype(jnp.float32) + 1.0

        def put(i, value):
            state_ref[i, z] = value

        post_collision(get, put, density, momentum(get), kind, por_ref[z], False)
        state_ref[POR, z] = por_ref[z]
        state_ref[KIND, z] = kind
        state_ref[WGT, z] = wgt_ref[z]
    slot_of = lanes() // (2 * HALO)
    for tile in range(EDGE_TILES):
        packed = jnp.zeros((YS, XS), jnp.float32)
        for slot in range(SLOTS):
            field, z = divmod(tile * SLOTS + slot, ZS)
            if field < FIELDS:
                moved = rot(state_ref[field, z], 2 * HALO * slot + HALO, 1)
                packed = jnp.where(slot_of == slot, moved, packed)
        edge_ref[tile] = packed


def rows_kernel(state_ref, odd_ref, even_ref, edge_ref, to_odd_ref, to_even_ref):
    from_left = (lanes() % (2 * HALO) < HALO).astype(jnp.int32)
    mine = (lax.axis_index("gx") % 2).astype(jnp.int32)
    for tile in range(EDGE_TILES):
        edge_ref[tile] = jnp.where(from_left == mine, even_ref[tile], odd_ref[tile])

    def pack(plan, start, ref):
        at = 0
        for field, z, row, rows in plan:
            ref[at : at + rows] = state_ref[field, z, row : row + rows]
            at += rows
        for tile in range(EDGE_TILES):
            at = ROWS_MAIN + HALO * tile
            ref[at : at + HALO] = edge_ref[tile, start : start + HALO]

    odd = parity("gy")

    @pl.when(odd)
    def _():
        pack(ROWS_LOW, 0, to_even_ref)
        pack(ROWS_HIGH, HALO, to_odd_ref)

    @pl.when(jnp.logical_not(odd))
    def _():
        pack(ROWS_HIGH, HALO, to_even_ref)
        pack(ROWS_LOW, 0, to_odd_ref)


def planes_kernel(state_ref, edge_ref, odd_ref, even_ref, wide_ref, side_ref, to_odd_ref, to_even_ref):
    for field in range(FIELDS):
        for z in range(ZS):
            wide_ref[field, z, 0] = state_ref[field, z]
    for tile in range(EDGE_TILES):
        side_ref[tile, 0] = edge_ref[tile]

    def unpack(plan, start, ref):
        at = 0
        for field, z, row, rows in plan:
            wide_ref[field, z, 1, row : row + rows] = ref[at : at + rows]
            at += rows
        for tile in range(EDGE_TILES):
            at = ROWS_MAIN + HALO * tile
            side_ref[tile, 1, start : start + HALO] = ref[at : at + HALO]

    odd = parity("gy")

    @pl.when(odd)
    def _():
        unpack(ROWS_HIGH, HALO, even_ref)
        unpack(ROWS_LOW, 0, odd_ref)

    @pl.when(jnp.logical_not(odd))
    def _():
        unpack(ROWS_LOW, 0, even_ref)
        unpack(ROWS_HIGH, HALO, odd_ref)

    def pack(plan, ref):
        for at, (field, z) in enumerate(plan):
            ref[at] = wide_ref[field, z]
        for tile in range(EDGE_TILES):
            ref[len(plan) + tile] = side_ref[tile]

    odd_z = parity("gz")

    @pl.when(odd_z)
    def _():
        pack(DOWN, to_even_ref)
        pack(UP, to_odd_ref)

    @pl.when(jnp.logical_not(odd_z))
    def _():
        pack(UP, to_even_ref)
        pack(DOWN, to_odd_ref)


def join(main, packed, slot):
    main = main.reshape(2 * YS, XS)
    side = rot(packed.reshape(2 * YS, XS), XS - HALO - 2 * HALO * slot, 1)
    return jnp.concatenate([main, side], axis=1)


def forward_kernel(scale, wide_ref, side_ref, odd_ref, even_ref, aux_ref, flow_ref, part_ref, f_ref):
    odd = parity("gz")

    def field_at(field, z):
        own = z % ZS
        tile, slot = divmod(field * ZS + own, SLOTS)
        if 0 <= z < ZS:
            return join(wide_ref[field, z], side_ref[tile], slot)
        plan = UP if z < 0 else DOWN
        main, side = plan.index((field, own)), len(plan) + tile
        first, second = (even_ref, odd_ref) if z < 0 else (odd_ref, even_ref)
        return join(
            jnp.where(odd, first[main], second[main]),
            jnp.where(odd, first[side], second[side]),
            slot,
        )

    for z in range(-1, ZS + 1):
        at = z + 1
        density = None
        moment = [None, None, None]
        for c in range(19):
            cx, cy, cz = DIRS[c]
            value = rot(rot(field_at(c, z - cz), cy, 0), cx, 1)
            f_ref[c, at] = value
            density = value if density is None else density + value
        get = lambda i: f_ref[i, at]
        moment = momentum(get)
        porosity, kind = field_at(POR, z), field_at(KIND, z)
        for axis in range(3):
            aux_ref[axis, at] = moment[axis]
        aux_ref[3, at] = porosity
        aux_ref[4, at] = kind

        def put(i, value):
            f_ref[i, at] = value

        wanted = [i for i in range(1, 19) if 0 <= z + DIRS[i][2] < ZS]
        post_collision(get, put, density, moment, kind, porosity, True, wanted)

    partial = jnp.zeros((YS, XS), jnp.float32)
    slot_of = lax.broadcasted_iota(jnp.int32, (2 * YS, XS), 1) // (2 * HALO)
    packed = jnp.zeros((2 * YS, XS), jnp.float32)
    for z in range(ZS):
        def arrived(i):
            cx, cy, cz = DIRS[i]
            return rot(rot(f_ref[i, z - cz + 1], cy, 0), cx, 1)

        moment = momentum(arrived)
        weight = field_at(WGT, z)
        for axis in range(3):
            flow = weight * moment[axis]
            partial = partial + flow[:YS, :XS] * moment[axis][:YS, :XS]
            slot = axis * ZS + z
            flow_ref[slot] = flow[:, :XS].reshape(2, YS, XS)
            moved = rot(flow[:, XS:], 2 * HALO * slot + HALO, 1)
            packed = jnp.where(slot_of == slot, moved, packed)
    flow_ref[3 * ZS] = packed.reshape(2, YS, XS)
    total = scale * jnp.sum(partial, axis=0, keepdims=True)
    part_ref[...] = jnp.broadcast_to(total[None], part_ref.shape)


def backward_kernel(
    flow_ref, odd_ref, even_ref, aux_ref, f_ref, por_ref, kind_ref, adjoint_ref, share_ref, g_ref
):
    odd = parity("gz")

    def flow_at(axis, z):
        slot = axis * ZS + z % ZS
        if 0 <= z < ZS:
            return join(flow_ref[slot], flow_ref[3 * ZS], slot)
        first, second = (even_ref, odd_ref) if z < 0 else (odd_ref, even_ref)
        return join(
            jnp.where(odd, first[slot], second[slot]),
            jnp.where(odd, first[3 * ZS], second[3 * ZS]),
            slot,
        )

    flows = [[flow_at(axis, z) for axis in range(3)] for z in range(-2, ZS + 2)]
    shares = []
    for z in range(-1, ZS + 1):
        at = z + 1
        g_ref[0, at] = jnp.zeros((2 * YS, 2 * XS), jnp.float32)
        for i in range(1, 19):
            cx, cy, cz = DIRS[i]
            seed = signed_sum(DIRS[i], flows[z + cz + 2])
            g_ref[i, at] = rot(rot(seed, -cy, 0), -cx, 1)
        get = lambda i: g_ref[i, at]

        def put(i, value):
            g_ref[i, at] = value

        moment = [aux_ref[axis, at] for axis in range(3)]
        wanted = [i for i in range(19) if 0 <= z - DIRS[i][2] < ZS]
        share = adjoint_collision(get, put, moment, aux_ref[4, at], aux_ref[3, at], True, wanted)
        if 0 <= z < ZS:
            shares.append(share[:YS, :XS])
    for z in range(ZS):
        for i in range(19):
            cx, cy, cz = DIRS[i]
            value = rot(g_ref[i, z + cz + 1], -cy, 0)[:YS]
            adjoint_ref[i, z] = rot(value, -cx, 1)[:, :XS]
        carried = lambda i: adjoint_ref[i, z]

        def put_out(i, value):
            adjoint_ref[i, z] = value

        moment = momentum(lambda i: f_ref[i, z])
        kind = kind_ref[z].astype(jnp.float32) + 1.0
        share = adjoint_collision(carried, put_out, moment, kind, por_ref[z], False)
        share_ref[z] = shares[z] + share


def spread_kernel(in_ref, out_ref):
    out_ref[...] = jnp.broadcast_to(jnp.sum(in_ref[...], axis=0, keepdims=True), out_ref.shape)


def call(kernel, outs, scratch=(), **options):
    shapes = tuple(jax.ShapeDtypeStruct(shape, jnp.float32) for shape in outs)
    return pl.pallas_call(
        kernel,
        out_shape=shapes if len(shapes) > 1 else shapes[0],
        scratch_shapes=[
            pltpu.VMEM(shape, jnp.float32) if isinstance(shape, tuple) else shape for shape in scratch
        ],
        compiler_params=pltpu.CompilerParams(vmem_limit_bytes=VMEM_LIMIT),
        **options,
    )


def swap(axis, to_even, to_odd, even_first=False):
    count = lax.axis_size(axis)

    def partners(first):
        return [
            pair for low in range(first, count - 1, 2) for pair in ((low, low + 1), (low + 1, low))
        ]

    if even_first:
        even = lax.ppermute(to_even, axis, partners(0))
        odd = lax.ppermute(to_odd, axis, partners(1))
    else:
        odd = lax.ppermute(to_odd, axis, partners(1))
        even = lax.ppermute(to_even, axis, partners(0))
    return odd, even


def columns():
    sizes = [lax.axis_size(axis) for axis in ("gx", "gy", "gz")]
    places = [(x, y) for x in range(sizes[0]) for y in range(sizes[1])]
    places.sort(key=lambda place: (place[1] // 4 * sizes[0] + place[0], place[1] % 4), reverse=True)
    return [[(x * sizes[1] + y) * sizes[2] + z for x, y in places] for z in range(sizes[2])]


def per_device(checkpoint, porosity, cell_kind, objective_weight):
    brick = (ZS, YS, XS)
    state, edge = call(
        edges_kernel,
        [(FIELDS,) + brick, (EDGE_TILES, YS, XS)],
        [(19,) + brick, brick, pltpu.VMEM(brick, jnp.int32), brick, pltpu.SemaphoreType.DMA((4,))],
        in_specs=[pl.BlockSpec(memory_space=pl.ANY)] * 4,
    )(
        *(
            pltpu.with_memory_space_constraint(value, pltpu.HBM)
            for value in (checkpoint, porosity, cell_kind, objective_weight)
        )
    )
    rows = (ROWS_MSG, XS)
    edge, to_odd, to_even = call(rows_kernel, [(EDGE_TILES, YS, XS), rows, rows])(
        state, *swap("gx", edge, edge)
    )
    planes = (ZMSG, 2, YS, XS)
    wide, side, to_odd, to_even = call(
        planes_kernel, [(FIELDS, ZS, 2, YS, XS), (EDGE_TILES, 2, YS, XS), planes, planes]
    )(state, edge, *swap("gy", to_even, to_odd))
    field = (ZS + 2, 2 * YS, 2 * XS)
    group = lax.axis_size("gz")
    plane = lax.axis_size("gx") * lax.axis_size("gy")
    cells = group * plane * ZS * YS * XS
    aux, flow, part = call(
        functools.partial(forward_kernel, 0.5 / cells),
        [(5,) + field, (3 * ZS + 1, 2, YS, XS), (group, 1, XS)],
        [(19,) + field],
    )(wide, side, *swap("gz", to_even, to_odd))
    flow_odd, flow_even = swap("gz", flow, flow, True)
    part = lax.all_to_all(part, "gz", 0, 0, tiled=True)
    part = call(spread_kernel, [(plane, 1, XS)])(part)
    part = lax.all_to_all(
        part, ("gx", "gy", "gz"), 0, 0, axis_index_groups=columns(), tiled=True
    )
    objective = jnp.sum(part)
    adjoint, share = call(backward_kernel, [(19,) + brick, brick], [(19,) + field])(
        flow, flow_odd, flow_even, aux, checkpoint, porosity, cell_kind
    )
    return adjoint, share, objective


def solution(mesh):
    cells = P("gz", "gy", "gx")
    populations = P(None, "gz", "gy", "gx")
    return jax.shard_map(
        per_device,
        mesh=mesh,
        in_specs=(populations, cells, cells, cells),
        out_specs=(populations, cells, P()),
        check_vma=False,
    )
```

```python
import functools

import jax
import jax.numpy as jnp
import numpy as np
from jax import lax
from jax.experimental import pallas as pl
from jax.experimental.pallas import tpu as pltpu
from jax.sharding import PartitionSpec as P

DIRS = (
    (0, 0, 0),
    (1, 0, 0), (-1, 0, 0), (0, 1, 0), (0, -1, 0), (0, 0, 1), (0, 0, -1),
    (1, 1, 0), (-1, -1, 0), (1, -1, 0), (-1, 1, 0),
    (1, 0, 1), (-1, 0, -1), (1, 0, -1), (-1, 0, 1),
    (0, 1, 1), (0, -1, -1), (0, 1, -1), (0, -1, 1),
)
WEIGHTS = tuple(float(np.float32(w)) for w in [1.0 / 3.0] + [1.0 / 18.0] * 6 + [1.0 / 36.0] * 12)
PAIRS = tuple((i, i + 1) for i in range(1, 19, 2))
RELAX = 1.25
INFLOW = (0.08, 0.0, 0.03)

ZS, YS, XS = 2, 8, 128
HALO = 4
POR, KIND, WGT, FIELDS = 19, 20, 21, 22
SLOTS = XS // (2 * HALO)
EDGE_TILES = -(-FIELDS * ZS // SLOTS)

UP = tuple((c, 0) for c in range(19) if DIRS[c][2] == 1) + tuple(
    (c, 1) for c in range(19) if DIRS[c][2] >= 0
) + ((POR, 1), (KIND, 1))
DOWN = tuple((c, 1) for c in range(19) if DIRS[c][2] == -1) + tuple(
    (c, 0) for c in range(19) if DIRS[c][2] <= 0
) + ((POR, 0), (KIND, 0))
ZMSG = len(UP) + EDGE_TILES


def row_plan(sign, order):
    plan = []
    first = min(order[0], order[1])
    for field in range(FIELDS):
        for z in range(ZS):
            plan.append((field, z, first, 2))
    for z in range(ZS):
        for field in range(WGT):
            if field >= POR or DIRS[field][1] in (0, sign):
                plan.append((field, z, order[2], 1))
    for z in range(ZS):
        for field in range(19):
            if DIRS[field][1] == sign:
                plan.append((field, z, order[3], 1))
    return tuple(plan)


ROWS_LOW = row_plan(-1, (0, 1, 2, 3))
ROWS_HIGH = row_plan(1, (7, 6, 5, 4))
ROWS_MAIN = sum(rows for _, _, _, rows in ROWS_LOW)
ROWS_MSG = -(-(ROWS_MAIN + HALO * EDGE_TILES) // 8) * 8

VMEM_LIMIT = 48 * 1024 * 1024


def rot(value, shift, axis):
    shift = shift % value.shape[axis]
    return value if shift == 0 else pltpu.roll(value, shift, axis)


def lanes():
    return lax.broadcasted_iota(jnp.int32, (YS, XS), 1)


def signed_sum(vector, parts):
    total = None
    for sign, part in zip(vector, parts):
        if sign == 0:
            continue
        if total is None:
            total = part if sign > 0 else -part
        else:
            total = total + part if sign > 0 else total - part
    return total


def momentum(get):
    parts = [None, None, None]
    for plus, minus in PAIRS:
        diff = get(plus) - get(minus)
        for axis in range(3):
            sign = DIRS[plus][axis]
            if sign:
                if parts[axis] is None:
                    parts[axis] = diff if sign > 0 else -diff
                else:
                    parts[axis] = parts[axis] + diff if sign > 0 else parts[axis] - diff
    return parts


def damping(kind, porosity):
    return jnp.where(kind == 2.0, 0.0, 1.0 - porosity)


def damped_of(moment, kind, scale):
    inlet = kind == 3.0
    return [
        scale * part + jnp.where(inlet, level, 0.0) if level else scale * part
        for part, level in zip(moment, INFLOW)
    ]


def post_collision(get, put, density, moment, kind, porosity, masked, wanted=range(19)):
    damped = damped_of(moment, kind, damping(kind, porosity))
    target = jnp.where(kind == 4.0, 1.0, density)
    square = damped[0] * damped[0] + damped[1] * damped[1] + damped[2] * damped[2]
    base = RELAX * (target - 1.5 * square)
    keep = 1.0 - RELAX
    if masked:
        inside = kind > 0.5
        base = jnp.where(inside, base, 0.0)
        damped = [jnp.where(inside, part, 0.0) for part in damped]
        keep = jnp.where(inside, keep, 0.0)
    if 0 in wanted:
        put(0, keep * get(0) + WEIGHTS[0] * base)
    for plus, minus in PAIRS:
        if plus not in wanted and minus not in wanted:
            continue
        weight = WEIGHTS[plus]
        along = signed_sum(DIRS[plus], damped)
        even = weight * base + (4.5 * RELAX * weight) * (along * along)
        odd = (3.0 * RELAX * weight) * along
        if plus in wanted:
            put(plus, keep * get(plus) + (even + odd))
        if minus in wanted:
            put(minus, keep * get(minus) + (even - odd))


def adjoint_collision(get, put, moment, kind, porosity, masked, wanted=range(19)):
    scale = damping(kind, porosity)
    damped = damped_of(moment, kind, scale)
    total = WEIGHTS[0] * get(0)
    slope = [None, None, None]
    for group in (PAIRS[:3], PAIRS[3:]):
        weight = WEIGHTS[group[0][0]]
        even_sum = None
        local = [None, None, None]
        for plus, minus in group:
            first, second = get(plus), get(minus)
            even, odd = first + second, first - second
            even_sum = even if even_sum is None else even_sum + even
            along = signed_sum(DIRS[plus], damped)
            term = odd + 3.0 * (along * even)
            for axis in range(3):
                sign = DIRS[plus][axis]
                if sign:
                    if local[axis] is None:
                        local[axis] = term if sign > 0 else -term
                    else:
                        local[axis] = local[axis] + term if sign > 0 else local[axis] - term
        total = total + weight * even_sum
        slope = [
            weight * new if old is None else old + weight * new for old, new in zip(slope, local)
        ]
    slope = [(3.0 * RELAX) * (part - total * drift) for part, drift in zip(slope, damped)]
    dot = slope[0] * moment[0] + slope[1] * moment[1] + slope[2] * moment[2]
    share = jnp.where(kind == 2.0, 0.0, -dot)
    even = jnp.where(kind == 4.0, 0.0, RELAX * total)
    back = [scale * part for part in slope]
    keep = 1.0 - RELAX
    if masked:
        inside = kind > 0.5
        even = jnp.where(inside, even, 0.0)
        back = [jnp.where(inside, part, 0.0) for part in back]
        keep = jnp.where(inside, keep, 0.0)
    if 0 in wanted:
        put(0, keep * get(0) + even)
    for plus, minus in PAIRS:
        if plus not in wanted and minus not in wanted:
            continue
        along = signed_sum(DIRS[plus], back)
        if plus in wanted:
            put(plus, keep * get(plus) + (even + along))
        if minus in wanted:
            put(minus, keep * get(minus) + (even - along))
    return share


def parity(axis):
    return lax.axis_index(axis) % 2 == 1


def edges_kernel(f_hbm, por_hbm, kind_hbm, wgt_hbm, state_ref, edge_ref, f_ref, por_ref, kind_ref, wgt_ref, sems):
    copies = [
        pltpu.make_async_copy(source, target, sems.at[at])
        for at, (source, target) in enumerate(
            ((f_hbm, f_ref), (por_hbm, por_ref), (kind_hbm, kind_ref), (wgt_hbm, wgt_ref))
        )
    ]
    for copy in copies:
        copy.start()
    for copy in copies:
        copy.wait()
    for z in range(ZS):
        get = lambda i: f_ref[i, z]
        density = functools.reduce(lambda a, b: a + b, [get(i) for i in range(19)])
        kind = kind_ref[z].astype(jnp.float32) + 1.0

        def put(i, value):
            state_ref[i, z] = value

        post_collision(get, put, density, momentum(get), kind, por_ref[z], False)
        state_ref[POR, z] = por_ref[z]
        state_ref[KIND, z] = kind
        state_ref[WGT, z] = wgt_ref[z]
    slot_of = lanes() // (2 * HALO)
    for tile in range(EDGE_TILES):
        packed = jnp.zeros((YS, XS), jnp.float32)
        for slot in range(SLOTS):
            field, z = divmod(tile * SLOTS + slot, ZS)
            if field < FIELDS:
                moved = rot(state_ref[field, z], 2 * HALO * slot + HALO, 1)
                packed = jnp.where(slot_of == slot, moved, packed)
        edge_ref[tile] = packed


def rows_kernel(state_ref, odd_ref, even_ref, edge_ref, to_odd_ref, to_even_ref):
    from_left = (lanes() % (2 * HALO) < HALO).astype(jnp.int32)
    mine = (lax.axis_index("gx") % 2).astype(jnp.int32)
    for tile in range(EDGE_TILES):
        edge_ref[tile] = jnp.where(from_left == mine, even_ref[tile], odd_ref[tile])

    def pack(plan, start, ref):
        at = 0
        for field, z, row, rows in plan:
            ref[at : at + rows] = state_ref[field, z, row : row + rows]
            at += rows
        for tile in range(EDGE_TILES):
            at = ROWS_MAIN + HALO * tile
            ref[at : at + HALO] = edge_ref[tile, start : start + HALO]

    odd = parity("gy")

    @pl.when(odd)
    def _():
        pack(ROWS_LOW, 0, to_even_ref)
        pack(ROWS_HIGH, HALO, to_odd_ref)

    @pl.when(jnp.logical_not(odd))
    def _():
        pack(ROWS_HIGH, HALO, to_even_ref)
        pack(ROWS_LOW, 0, to_odd_ref)


def planes_kernel(state_ref, edge_ref, odd_ref, even_ref, wide_ref, side_ref, to_odd_ref, to_even_ref):
    for field in range(FIELDS):
        for z in range(ZS):
            wide_ref[field, z, 0] = state_ref[field, z]
    for tile in range(EDGE_TILES):
        side_ref[tile, 0] = edge_ref[tile]

    def unpack(plan, start, ref):
        at = 0
        for field, z, row, rows in plan:
            wide_ref[field, z, 1, row : row + rows] = ref[at : at + rows]
            at += rows
        for tile in range(EDGE_TILES):
            at = ROWS_MAIN + HALO * tile
            side_ref[tile, 1, start : start + HALO] = ref[at : at + HALO]

    odd = parity("gy")

    @pl.when(odd)
    def _():
        unpack(ROWS_HIGH, HALO, even_ref)
        unpack(ROWS_LOW, 0, odd_ref)

    @pl.when(jnp.logical_not(odd))
    def _():
        unpack(ROWS_LOW, 0, even_ref)
        unpack(ROWS_HIGH, HALO, odd_ref)

    def pack(plan, ref):
        for at, (field, z) in enumerate(plan):
            ref[at] = wide_ref[field, z]
        for tile in range(EDGE_TILES):
            ref[len(plan) + tile] = side_ref[tile]

    odd_z = parity("gz")

    @pl.when(odd_z)
    def _():
        pack(DOWN, to_even_ref)
        pack(UP, to_odd_ref)

    @pl.when(jnp.logical_not(odd_z))
    def _():
        pack(UP, to_even_ref)
        pack(DOWN, to_odd_ref)


def join(main, packed, slot):
    main = main.reshape(2 * YS, XS)
    side = rot(packed.reshape(2 * YS, XS), XS - HALO - 2 * HALO * slot, 1)
    return jnp.concatenate([main, side], axis=1)


def forward_kernel(scale, wide_ref, side_ref, odd_ref, even_ref, aux_ref, flow_ref, part_ref, f_ref):
    odd = parity("gz")

    def field_at(field, z):
        own = z % ZS
        tile, slot = divmod(field * ZS + own, SLOTS)
        if 0 <= z < ZS:
            return join(wide_ref[field, z], side_ref[tile], slot)
        plan = UP if z < 0 else DOWN
        main, side = plan.index((field, own)), len(plan) + tile
        first, second = (even_ref, odd_ref) if z < 0 else (odd_ref, even_ref)
        return join(
            jnp.where(odd, first[main], second[main]),
            jnp.where(odd, first[side], second[side]),
            slot,
        )

    for z in range(-1, ZS + 1):
        at = z + 1
        density = None
        moment = [None, None, None]
        for c in range(19):
            cx, cy, cz = DIRS[c]
            value = rot(rot(field_at(c, z - cz), cy, 0), cx, 1)
            f_ref[c, at] = value
            density = value if density is None else density + value
        get = lambda i: f_ref[i, at]
        moment = momentum(get)
        porosity, kind = field_at(POR, z), field_at(KIND, z)
        for axis in range(3):
            aux_ref[axis, at] = moment[axis]
        aux_ref[3, at] = porosity
        aux_ref[4, at] = kind

        def put(i, value):
            f_ref[i, at] = value

        wanted = [i for i in range(1, 19) if 0 <= z + DIRS[i][2] < ZS]
        post_collision(get, put, density, moment, kind, porosity, True, wanted)

    partial = jnp.zeros((YS, XS), jnp.float32)
    slot_of = lax.broadcasted_iota(jnp.int32, (2 * YS, XS), 1) // (2 * HALO)
    packed = jnp.zeros((2 * YS, XS), jnp.float32)
    for z in range(ZS):
        def arrived(i):
            cx, cy, cz = DIRS[i]
            return rot(rot(f_ref[i, z - cz + 1], cy, 0), cx, 1)

        moment = momentum(arrived)
        weight = field_at(WGT, z)
        for axis in range(3):
            flow = weight * moment[axis]
            partial = partial + flow[:YS, :XS] * moment[axis][:YS, :XS]
            slot = axis * ZS + z
            flow_ref[slot] = flow[:, :XS].reshape(2, YS, XS)
            moved = rot(flow[:, XS:], 2 * HALO * slot + HALO, 1)
            packed = jnp.where(slot_of == slot, moved, packed)
    flow_ref[3 * ZS] = packed.reshape(2, YS, XS)
    total = scale * jnp.sum(partial, axis=0, keepdims=True)
    part_ref[...] = jnp.broadcast_to(total[None], part_ref.shape)


def backward_kernel(
    flow_ref, even_ref, odd_ref, aux_ref, f_ref, por_ref, kind_ref, adjoint_ref, share_ref, g_ref
):
    odd = parity("gz")

    def flow_at(axis, z):
        slot = axis * ZS + z % ZS
        if 0 <= z < ZS:
            return join(flow_ref[slot], flow_ref[3 * ZS], slot)
        first, second = (even_ref, odd_ref) if z < 0 else (odd_ref, even_ref)
        return join(
            jnp.where(odd, first[slot], second[slot]),
            jnp.where(odd, first[3 * ZS], second[3 * ZS]),
            slot,
        )

    flows = [[flow_at(axis, z) for axis in range(3)] for z in range(-2, ZS + 2)]
    shares = []
    for z in range(-1, ZS + 1):
        at = z + 1
        g_ref[0, at] = jnp.zeros((2 * YS, 2 * XS), jnp.float32)
        for i in range(1, 19):
            cx, cy, cz = DIRS[i]
            seed = signed_sum(DIRS[i], flows[z + cz + 2])
            g_ref[i, at] = rot(rot(seed, -cy, 0), -cx, 1)
        get = lambda i: g_ref[i, at]

        def put(i, value):
            g_ref[i, at] = value

        moment = [aux_ref[axis, at] for axis in range(3)]
        wanted = [i for i in range(19) if 0 <= z - DIRS[i][2] < ZS]
        share = adjoint_collision(get, put, moment, aux_ref[4, at], aux_ref[3, at], True, wanted)
        if 0 <= z < ZS:
            shares.append(share[:YS, :XS])
    for z in range(ZS):
        for i in range(19):
            cx, cy, cz = DIRS[i]
            value = rot(g_ref[i, z + cz + 1], -cy, 0)[:YS]
            adjoint_ref[i, z] = rot(value, -cx, 1)[:, :XS]
        carried = lambda i: adjoint_ref[i, z]

        def put_out(i, value):
            adjoint_ref[i, z] = value

        moment = momentum(lambda i: f_ref[i, z])
        kind = kind_ref[z].astype(jnp.float32) + 1.0
        share = adjoint_collision(carried, put_out, moment, kind, por_ref[z], False)
        share_ref[z] = shares[z] + share


def spread_kernel(in_ref, out_ref):
    out_ref[...] = jnp.broadcast_to(jnp.sum(in_ref[...], axis=0, keepdims=True), out_ref.shape)


def call(kernel, outs, scratch=(), **options):
    shapes = tuple(jax.ShapeDtypeStruct(shape, jnp.float32) for shape in outs)
    return pl.pallas_call(
        kernel,
        out_shape=shapes if len(shapes) > 1 else shapes[0],
        scratch_shapes=[
            pltpu.VMEM(shape, jnp.float32) if isinstance(shape, tuple) else shape for shape in scratch
        ],
        compiler_params=pltpu.CompilerParams(vmem_limit_bytes=VMEM_LIMIT),
        **options,
    )


def swap(axis, to_even, to_odd, even_first=False):
    count = lax.axis_size(axis)

    def partners(first):
        return [
            pair for low in range(first, count - 1, 2) for pair in ((low, low + 1), (low + 1, low))
        ]

    if even_first:
        even = lax.ppermute(to_even, axis, partners(0))
        odd = lax.ppermute(to_odd, axis, partners(1))
    else:
        odd = lax.ppermute(to_odd, axis, partners(1))
        even = lax.ppermute(to_even, axis, partners(0))
    return odd, even


def columns():
    sizes = [lax.axis_size(axis) for axis in ("gx", "gy", "gz")]
    places = [(x, y) for x in range(sizes[0]) for y in range(sizes[1])]
    places.sort(key=lambda place: (place[1] // 4 * sizes[0] + place[0], place[1] % 4), reverse=True)
    turn = len(places) // 8
    places = places[turn:] + places[:turn]
    return [[(x * sizes[1] + y) * sizes[2] + z for x, y in places] for z in range(sizes[2])]


def per_device(checkpoint, porosity, cell_kind, objective_weight):
    brick = (ZS, YS, XS)
    state, edge = call(
        edges_kernel,
        [(FIELDS,) + brick, (EDGE_TILES, YS, XS)],
        [(19,) + brick, brick, pltpu.VMEM(brick, jnp.int32), brick, pltpu.SemaphoreType.DMA((4,))],
        in_specs=[pl.BlockSpec(memory_space=pl.ANY)] * 4,
    )(
        *(
            pltpu.with_memory_space_constraint(value, pltpu.HBM)
            for value in (checkpoint, porosity, cell_kind, objective_weight)
        )
    )
    rows = (ROWS_MSG, XS)
    edge, to_odd, to_even = call(rows_kernel, [(EDGE_TILES, YS, XS), rows, rows])(
        state, *swap("gx", edge, edge)
    )
    planes = (ZMSG, 2, YS, XS)
    wide, side, to_odd, to_even = call(
        planes_kernel, [(FIELDS, ZS, 2, YS, XS), (EDGE_TILES, 2, YS, XS), planes, planes]
    )(state, edge, *swap("gy", to_even, to_odd))
    field = (ZS + 2, 2 * YS, 2 * XS)
    group = lax.axis_size("gz")
    plane = lax.axis_size("gx") * lax.axis_size("gy")
    cells = group * plane * ZS * YS * XS
    aux, flow, part = call(
        functools.partial(forward_kernel, 0.5 / cells),
        [(5,) + field, (3 * ZS + 1, 2, YS, XS), (group, 1, XS)],
        [(19,) + field],
    )(wide, side, *swap("gz", to_even, to_odd))
    flow_odd, flow_even = swap("gz", flow, flow, True)
    part = lax.all_to_all(part, "gz", 0, 0, tiled=True)
    part = call(spread_kernel, [(plane, 1, XS)])(part)
    part = lax.all_to_all(
        part, ("gx", "gy", "gz"), 0, 0, axis_index_groups=columns(), tiled=True
    )
    objective = jnp.sum(part)
    adjoint, share = call(backward_kernel, [(19,) + brick, brick], [(19,) + field])(
        flow, flow_even, flow_odd, aux, checkpoint, porosity, cell_kind
    )
    return adjoint, share, objective


def solution(mesh):
    cells = P("gz", "gy", "gx")
    populations = P(None, "gz", "gy", "gx")
    return jax.shard_map(
        per_device,
        mesh=mesh,
        in_specs=(populations, cells, cells, cells),
        out_specs=(populations, cells, P()),
        check_vma=False,
    )
```

```python
import functools

import jax
import jax.numpy as jnp
import numpy as np
from jax import lax
from jax.experimental import pallas as pl
from jax.experimental.pallas import tpu as pltpu
from jax.sharding import PartitionSpec as P

DIRS = (
    (0, 0, 0),
    (1, 0, 0), (-1, 0, 0), (0, 1, 0), (0, -1, 0), (0, 0, 1), (0, 0, -1),
    (1, 1, 0), (-1, -1, 0), (1, -1, 0), (-1, 1, 0),
    (1, 0, 1), (-1, 0, -1), (1, 0, -1), (-1, 0, 1),
    (0, 1, 1), (0, -1, -1), (0, 1, -1), (0, -1, 1),
)
WEIGHTS = tuple(float(np.float32(w)) for w in [1.0 / 3.0] + [1.0 / 18.0] * 6 + [1.0 / 36.0] * 12)
PAIRS = tuple((i, i + 1) for i in range(1, 19, 2))
RELAX = 1.25
INFLOW = (0.08, 0.0, 0.03)

ZS, YS, XS = 2, 8, 128
HALO = 4
POR, KIND, WGT, FIELDS = 19, 20, 21, 22
SLOTS = XS // (2 * HALO)
EDGE_TILES = -(-FIELDS * ZS // SLOTS)

UP = tuple((c, 0) for c in range(19) if DIRS[c][2] == 1) + tuple(
    (c, 1) for c in range(19) if DIRS[c][2] >= 0
) + ((POR, 1), (KIND, 1))
DOWN = tuple((c, 1) for c in range(19) if DIRS[c][2] == -1) + tuple(
    (c, 0) for c in range(19) if DIRS[c][2] <= 0
) + ((POR, 0), (KIND, 0))
ZMSG = len(UP) + EDGE_TILES


def row_plan(sign, order):
    plan = []
    first = min(order[0], order[1])
    for field in range(FIELDS):
        for z in range(ZS):
            plan.append((field, z, first, 2))
    for z in range(ZS):
        for field in range(WGT):
            if field >= POR or DIRS[field][1] in (0, sign):
                plan.append((field, z, order[2], 1))
    for z in range(ZS):
        for field in range(19):
            if DIRS[field][1] == sign:
                plan.append((field, z, order[3], 1))
    return tuple(plan)


ROWS_LOW = row_plan(-1, (0, 1, 2, 3))
ROWS_HIGH = row_plan(1, (7, 6, 5, 4))
ROWS_MAIN = sum(rows for _, _, _, rows in ROWS_LOW)
ROWS_MSG = -(-(ROWS_MAIN + HALO * EDGE_TILES) // 8) * 8

VMEM_LIMIT = 48 * 1024 * 1024


def rot(value, shift, axis):
    shift = shift % value.shape[axis]
    return value if shift == 0 else pltpu.roll(value, shift, axis)


def lanes():
    return lax.broadcasted_iota(jnp.int32, (YS, XS), 1)


def signed_sum(vector, parts):
    total = None
    for sign, part in zip(vector, parts):
        if sign == 0:
            continue
        if total is None:
            total = part if sign > 0 else -part
        else:
            total = total + part if sign > 0 else total - part
    return total


def momentum(get):
    parts = [None, None, None]
    for plus, minus in PAIRS:
        diff = get(plus) - get(minus)
        for axis in range(3):
            sign = DIRS[plus][axis]
            if sign:
                if parts[axis] is None:
                    parts[axis] = diff if sign > 0 else -diff
                else:
                    parts[axis] = parts[axis] + diff if sign > 0 else parts[axis] - diff
    return parts


def damping(kind, porosity):
    return jnp.where(kind == 2.0, 0.0, 1.0 - porosity)


def damped_of(moment, kind, scale):
    inlet = kind == 3.0
    return [
        scale * part + jnp.where(inlet, level, 0.0) if level else scale * part
        for part, level in zip(moment, INFLOW)
    ]


def post_collision(get, put, density, moment, kind, porosity, masked, wanted=range(19)):
    damped = damped_of(moment, kind, damping(kind, porosity))
    target = jnp.where(kind == 4.0, 1.0, density)
    square = damped[0] * damped[0] + damped[1] * damped[1] + damped[2] * damped[2]
    base = RELAX * (target - 1.5 * square)
    keep = 1.0 - RELAX
    if masked:
        inside = kind > 0.5
        base = jnp.where(inside, base, 0.0)
        damped = [jnp.where(inside, part, 0.0) for part in damped]
        keep = jnp.where(inside, keep, 0.0)
    if 0 in wanted:
        put(0, keep * get(0) + WEIGHTS[0] * base)
    for plus, minus in PAIRS:
        if plus not in wanted and minus not in wanted:
            continue
        weight = WEIGHTS[plus]
        along = signed_sum(DIRS[plus], damped)
        even = weight * base + (4.5 * RELAX * weight) * (along * along)
        odd = (3.0 * RELAX * weight) * along
        if plus in wanted:
            put(plus, keep * get(plus) + (even + odd))
        if minus in wanted:
            put(minus, keep * get(minus) + (even - odd))


def adjoint_collision(get, put, moment, kind, porosity, masked, wanted=range(19)):
    scale = damping(kind, porosity)
    damped = damped_of(moment, kind, scale)
    total = WEIGHTS[0] * get(0)
    slope = [None, None, None]
    for group in (PAIRS[:3], PAIRS[3:]):
        weight = WEIGHTS[group[0][0]]
        even_sum = None
        local = [None, None, None]
        for plus, minus in group:
            first, second = get(plus), get(minus)
            even, odd = first + second, first - second
            even_sum = even if even_sum is None else even_sum + even
            along = signed_sum(DIRS[plus], damped)
            term = odd + 3.0 * (along * even)
            for axis in range(3):
                sign = DIRS[plus][axis]
                if sign:
                    if local[axis] is None:
                        local[axis] = term if sign > 0 else -term
                    else:
                        local[axis] = local[axis] + term if sign > 0 else local[axis] - term
        total = total + weight * even_sum
        slope = [
            weight * new if old is None else old + weight * new for old, new in zip(slope, local)
        ]
    slope = [(3.0 * RELAX) * (part - total * drift) for part, drift in zip(slope, damped)]
    dot = slope[0] * moment[0] + slope[1] * moment[1] + slope[2] * moment[2]
    share = jnp.where(kind == 2.0, 0.0, -dot)
    even = jnp.where(kind == 4.0, 0.0, RELAX * total)
    back = [scale * part for part in slope]
    keep = 1.0 - RELAX
    if masked:
        inside = kind > 0.5
        even = jnp.where(inside, even, 0.0)
        back = [jnp.where(inside, part, 0.0) for part in back]
        keep = jnp.where(inside, keep, 0.0)
    if 0 in wanted:
        put(0, keep * get(0) + even)
    for plus, minus in PAIRS:
        if plus not in wanted and minus not in wanted:
            continue
        along = signed_sum(DIRS[plus], back)
        if plus in wanted:
            put(plus, keep * get(plus) + (even + along))
        if minus in wanted:
            put(minus, keep * get(minus) + (even - along))
    return share


def parity(axis):
    return lax.axis_index(axis) % 2 == 1


def edges_kernel(f_hbm, por_hbm, kind_hbm, wgt_hbm, state_ref, edge_ref, f_ref, por_ref, kind_ref, wgt_ref, sems):
    copies = [
        pltpu.make_async_copy(source, target, sems.at[at])
        for at, (source, target) in enumerate(
            ((f_hbm, f_ref), (por_hbm, por_ref), (kind_hbm, kind_ref), (wgt_hbm, wgt_ref))
        )
    ]
    for copy in copies:
        copy.start()
    for copy in copies:
        copy.wait()
    for z in range(ZS):
        get = lambda i: f_ref[i, z]
        density = functools.reduce(lambda a, b: a + b, [get(i) for i in range(19)])
        kind = kind_ref[z].astype(jnp.float32) + 1.0

        def put(i, value):
            state_ref[i, z] = value

        post_collision(get, put, density, momentum(get), kind, por_ref[z], False)
        state_ref[POR, z] = por_ref[z]
        state_ref[KIND, z] = kind
        state_ref[WGT, z] = wgt_ref[z]
    slot_of = lanes() // (2 * HALO)
    for tile in range(EDGE_TILES):
        packed = jnp.zeros((YS, XS), jnp.float32)
        for slot in range(SLOTS):
            field, z = divmod(tile * SLOTS + slot, ZS)
            if field < FIELDS:
                moved = rot(state_ref[field, z], 2 * HALO * slot + HALO, 1)
                packed = jnp.where(slot_of == slot, moved, packed)
        edge_ref[tile] = packed


def rows_kernel(state_ref, odd_ref, even_ref, edge_ref, to_odd_ref, to_even_ref):
    from_left = (lanes() % (2 * HALO) < HALO).astype(jnp.int32)
    mine = (lax.axis_index("gx") % 2).astype(jnp.int32)
    for tile in range(EDGE_TILES):
        edge_ref[tile] = jnp.where(from_left == mine, even_ref[tile], odd_ref[tile])

    def pack(plan, start, ref):
        at = 0
        for field, z, row, rows in plan:
            ref[at : at + rows] = state_ref[field, z, row : row + rows]
            at += rows
        for tile in range(EDGE_TILES):
            at = ROWS_MAIN + HALO * tile
            ref[at : at + HALO] = edge_ref[tile, start : start + HALO]

    odd = parity("gy")

    @pl.when(odd)
    def _():
        pack(ROWS_LOW, 0, to_even_ref)
        pack(ROWS_HIGH, HALO, to_odd_ref)

    @pl.when(jnp.logical_not(odd))
    def _():
        pack(ROWS_HIGH, HALO, to_even_ref)
        pack(ROWS_LOW, 0, to_odd_ref)


def planes_kernel(state_ref, edge_ref, odd_ref, even_ref, wide_ref, side_ref, to_odd_ref, to_even_ref):
    for field in range(FIELDS):
        for z in range(ZS):
            wide_ref[field, z, 0] = state_ref[field, z]
    for tile in range(EDGE_TILES):
        side_ref[tile, 0] = edge_ref[tile]

    def unpack(plan, start, ref):
        at = 0
        for field, z, row, rows in plan:
            wide_ref[field, z, 1, row : row + rows] = ref[at : at + rows]
            at += rows
        for tile in range(EDGE_TILES):
            at = ROWS_MAIN + HALO * tile
            side_ref[tile, 1, start : start + HALO] = ref[at : at + HALO]

    odd = parity("gy")

    @pl.when(odd)
    def _():
        unpack(ROWS_HIGH, HALO, even_ref)
        unpack(ROWS_LOW, 0, odd_ref)

    @pl.when(jnp.logical_not(odd))
    def _():
        unpack(ROWS_LOW, 0, even_ref)
        unpack(ROWS_HIGH, HALO, odd_ref)

    def pack(plan, ref):
        for at, (field, z) in enumerate(plan):
            ref[at] = wide_ref[field, z]
        for tile in range(EDGE_TILES):
            ref[len(plan) + tile] = side_ref[tile]

    odd_z = parity("gz")

    @pl.when(odd_z)
    def _():
        pack(DOWN, to_even_ref)
        pack(UP, to_odd_ref)

    @pl.when(jnp.logical_not(odd_z))
    def _():
        pack(UP, to_even_ref)
        pack(DOWN, to_odd_ref)


def join(main, packed, slot):
    main = main.reshape(2 * YS, XS)
    side = rot(packed.reshape(2 * YS, XS), XS - HALO - 2 * HALO * slot, 1)
    return jnp.concatenate([main, side], axis=1)


def forward_kernel(scale, wide_ref, side_ref, odd_ref, even_ref, aux_ref, flow_ref, part_ref, f_ref):
    odd = parity("gz")

    def field_at(field, z):
        own = z % ZS
        tile, slot = divmod(field * ZS + own, SLOTS)
        if 0 <= z < ZS:
            return join(wide_ref[field, z], side_ref[tile], slot)
        plan = UP if z < 0 else DOWN
        main, side = plan.index((field, own)), len(plan) + tile
        first, second = (even_ref, odd_ref) if z < 0 else (odd_ref, even_ref)
        return join(
            jnp.where(odd, first[main], second[main]),
            jnp.where(odd, first[side], second[side]),
            slot,
        )

    for z in range(-1, ZS + 1):
        at = z + 1
        density = None
        moment = [None, None, None]
        for c in range(19):
            cx, cy, cz = DIRS[c]
            value = rot(rot(field_at(c, z - cz), cy, 0), cx, 1)
            f_ref[c, at] = value
            density = value if density is None else density + value
        get = lambda i: f_ref[i, at]
        moment = momentum(get)
        porosity, kind = field_at(POR, z), field_at(KIND, z)
        for axis in range(3):
            aux_ref[axis, at] = moment[axis]
        aux_ref[3, at] = porosity
        aux_ref[4, at] = kind

        def put(i, value):
            f_ref[i, at] = value

        wanted = [i for i in range(1, 19) if 0 <= z + DIRS[i][2] < ZS]
        post_collision(get, put, density, moment, kind, porosity, True, wanted)

    partial = jnp.zeros((YS, XS), jnp.float32)
    slot_of = lax.broadcasted_iota(jnp.int32, (2 * YS, XS), 1) // (2 * HALO)
    packed = jnp.zeros((2 * YS, XS), jnp.float32)
    for z in range(ZS):
        def arrived(i):
            cx, cy, cz = DIRS[i]
            return rot(rot(f_ref[i, z - cz + 1], cy, 0), cx, 1)

        moment = momentum(arrived)
        weight = field_at(WGT, z)
        for axis in range(3):
            flow = weight * moment[axis]
            partial = partial + flow[:YS, :XS] * moment[axis][:YS, :XS]
            slot = axis * ZS + z
            flow_ref[slot] = flow[:, :XS].reshape(2, YS, XS)
            moved = rot(flow[:, XS:], 2 * HALO * slot + HALO, 1)
            packed = jnp.where(slot_of == slot, moved, packed)
    flow_ref[3 * ZS] = packed.reshape(2, YS, XS)
    total = scale * jnp.sum(partial, axis=0, keepdims=True)
    part_ref[...] = jnp.broadcast_to(total[None], part_ref.shape)


def backward_kernel(
    flow_ref, even_ref, odd_ref, aux_ref, f_ref, por_ref, kind_ref, adjoint_ref, share_ref, g_ref
):
    odd = parity("gz")

    def flow_at(axis, z):
        slot = axis * ZS + z % ZS
        if 0 <= z < ZS:
            return join(flow_ref[slot], flow_ref[3 * ZS], slot)
        first, second = (even_ref, odd_ref) if z < 0 else (odd_ref, even_ref)
        return join(
            jnp.where(odd, first[slot], second[slot]),
            jnp.where(odd, first[3 * ZS], second[3 * ZS]),
            slot,
        )

    flows = [[flow_at(axis, z) for axis in range(3)] for z in range(-2, ZS + 2)]
    shares = []
    for z in range(-1, ZS + 1):
        at = z + 1
        g_ref[0, at] = jnp.zeros((2 * YS, 2 * XS), jnp.float32)
        for i in range(1, 19):
            cx, cy, cz = DIRS[i]
            seed = signed_sum(DIRS[i], flows[z + cz + 2])
            g_ref[i, at] = rot(rot(seed, -cy, 0), -cx, 1)
        get = lambda i: g_ref[i, at]

        def put(i, value):
            g_ref[i, at] = value

        moment = [aux_ref[axis, at] for axis in range(3)]
        wanted = [i for i in range(19) if 0 <= z - DIRS[i][2] < ZS]
        share = adjoint_collision(get, put, moment, aux_ref[4, at], aux_ref[3, at], True, wanted)
        if 0 <= z < ZS:
            shares.append(share[:YS, :XS])
    for z in range(ZS):
        for i in range(19):
            cx, cy, cz = DIRS[i]
            value = rot(g_ref[i, z + cz + 1], -cy, 0)[:YS]
            adjoint_ref[i, z] = rot(value, -cx, 1)[:, :XS]
        carried = lambda i: adjoint_ref[i, z]

        def put_out(i, value):
            adjoint_ref[i, z] = value

        moment = momentum(lambda i: f_ref[i, z])
        kind = kind_ref[z].astype(jnp.float32) + 1.0
        share = adjoint_collision(carried, put_out, moment, kind, por_ref[z], False)
        share_ref[z] = shares[z] + share


def spread_kernel(in_ref, out_ref):
    out_ref[...] = jnp.broadcast_to(jnp.sum(in_ref[...], axis=0, keepdims=True), out_ref.shape)


def call(kernel, outs, scratch=(), **options):
    shapes = tuple(jax.ShapeDtypeStruct(shape, jnp.float32) for shape in outs)
    return pl.pallas_call(
        kernel,
        out_shape=shapes if len(shapes) > 1 else shapes[0],
        scratch_shapes=[
            pltpu.VMEM(shape, jnp.float32) if isinstance(shape, tuple) else shape for shape in scratch
        ],
        compiler_params=pltpu.CompilerParams(vmem_limit_bytes=VMEM_LIMIT),
        **options,
    )


def swap(axis, to_even, to_odd, even_first=False):
    count = lax.axis_size(axis)

    def partners(first):
        return [
            pair for low in range(first, count - 1, 2) for pair in ((low, low + 1), (low + 1, low))
        ]

    if even_first:
        even = lax.ppermute(to_even, axis, partners(0))
        odd = lax.ppermute(to_odd, axis, partners(1))
    else:
        odd = lax.ppermute(to_odd, axis, partners(1))
        even = lax.ppermute(to_even, axis, partners(0))
    return odd, even


def columns():
    sizes = [lax.axis_size(axis) for axis in ("gx", "gy", "gz")]
    places = [(x, y) for x in range(sizes[0]) for y in range(sizes[1])]
    places.sort(key=lambda place: (place[1] // 4 * sizes[0] + place[0], place[1] % 4), reverse=True)
    turn = len(places) // 8
    places = places[turn:] + places[:turn]
    return [[(x * sizes[1] + y) * sizes[2] + z for x, y in places] for z in range(sizes[2])]


def per_device(checkpoint, porosity, cell_kind, objective_weight):
    brick = (ZS, YS, XS)
    state, edge = call(
        edges_kernel,
        [(FIELDS,) + brick, (EDGE_TILES, YS, XS)],
        [(19,) + brick, brick, pltpu.VMEM(brick, jnp.int32), brick, pltpu.SemaphoreType.DMA((4,))],
        in_specs=[pl.BlockSpec(memory_space=pl.ANY)] * 4,
    )(
        *(
            pltpu.with_memory_space_constraint(value, pltpu.HBM)
            for value in (checkpoint, porosity, cell_kind, objective_weight)
        )
    )
    rows = (ROWS_MSG, XS)
    edge, to_odd, to_even = call(rows_kernel, [(EDGE_TILES, YS, XS), rows, rows])(
        state, *swap("gx", edge, edge)
    )
    planes = (ZMSG, 2, YS, XS)
    wide, side, to_odd, to_even = call(
        planes_kernel, [(FIELDS, ZS, 2, YS, XS), (EDGE_TILES, 2, YS, XS), planes, planes]
    )(state, edge, *swap("gy", to_even, to_odd))
    field = (ZS + 2, 2 * YS, 2 * XS)
    group = lax.axis_size("gz")
    plane = lax.axis_size("gx") * lax.axis_size("gy")
    cells = group * plane * ZS * YS * XS
    aux, flow, part = call(
        functools.partial(forward_kernel, 0.5 / cells),
        [(5,) + field, (3 * ZS + 1, 2, YS, XS), (group, 1, XS)],
        [(19,) + field],
    )(wide, side, *swap("gz", to_even, to_odd))
    flow_odd, flow_even = swap("gz", flow, flow, True)
    falling = [list(range(group))[::-1]]
    part = lax.all_to_all(part, "gz", 0, 0, axis_index_groups=falling, tiled=True)
    part = call(spread_kernel, [(plane, 1, XS)])(part)
    part = lax.all_to_all(
        part, ("gx", "gy", "gz"), 0, 0, axis_index_groups=columns(), tiled=True
    )
    objective = jnp.sum(part)
    adjoint, share = call(backward_kernel, [(19,) + brick, brick], [(19,) + field])(
        flow, flow_even, flow_odd, aux, checkpoint, porosity, cell_kind
    )
    return adjoint, share, objective


def solution(mesh):
    cells = P("gz", "gy", "gx")
    populations = P(None, "gz", "gy", "gx")
    return jax.shard_map(
        per_device,
        mesh=mesh,
        in_specs=(populations, cells, cells, cells),
        out_specs=(populations, cells, P()),
        check_vma=False,
    )
```

```python
import functools

import jax
import jax.numpy as jnp
import numpy as np
from jax import lax
from jax.experimental import pallas as pl
from jax.experimental.pallas import tpu as pltpu
from jax.sharding import PartitionSpec as P

DIRS = (
    (0, 0, 0),
    (1, 0, 0), (-1, 0, 0), (0, 1, 0), (0, -1, 0), (0, 0, 1), (0, 0, -1),
    (1, 1, 0), (-1, -1, 0), (1, -1, 0), (-1, 1, 0),
    (1, 0, 1), (-1, 0, -1), (1, 0, -1), (-1, 0, 1),
    (0, 1, 1), (0, -1, -1), (0, 1, -1), (0, -1, 1),
)
WEIGHTS = tuple(float(np.float32(w)) for w in [1.0 / 3.0] + [1.0 / 18.0] * 6 + [1.0 / 36.0] * 12)
PAIRS = tuple((i, i + 1) for i in range(1, 19, 2))
RELAX = 1.25
INFLOW = (0.08, 0.0, 0.03)

ZS, YS, XS = 2, 8, 128
HALO = 4
POR, KIND, WGT, FIELDS = 19, 20, 21, 22
SLOTS = XS // (2 * HALO)
EDGE_TILES = -(-FIELDS * ZS // SLOTS)

UP = tuple((c, 0) for c in range(19) if DIRS[c][2] == 1) + tuple(
    (c, 1) for c in range(19) if DIRS[c][2] >= 0
) + ((POR, 1), (KIND, 1))
DOWN = tuple((c, 1) for c in range(19) if DIRS[c][2] == -1) + tuple(
    (c, 0) for c in range(19) if DIRS[c][2] <= 0
) + ((POR, 0), (KIND, 0))
ZMSG = len(UP) + EDGE_TILES


def row_plan(sign, order):
    plan = []
    first = min(order[0], order[1])
    for field in range(FIELDS):
        for z in range(ZS):
            plan.append((field, z, first, 2))
    for z in range(ZS):
        for field in range(WGT):
            if field >= POR or DIRS[field][1] in (0, sign):
                plan.append((field, z, order[2], 1))
    for z in range(ZS):
        for field in range(19):
            if DIRS[field][1] == sign:
                plan.append((field, z, order[3], 1))
    return tuple(plan)


ROWS_LOW = row_plan(-1, (0, 1, 2, 3))
ROWS_HIGH = row_plan(1, (7, 6, 5, 4))
ROWS_MAIN = sum(rows for _, _, _, rows in ROWS_LOW)
ROWS_MSG = -(-(ROWS_MAIN + HALO * EDGE_TILES) // 8) * 8

VMEM_LIMIT = 48 * 1024 * 1024


def rot(value, shift, axis):
    shift = shift % value.shape[axis]
    return value if shift == 0 else pltpu.roll(value, shift, axis)


def lanes():
    return lax.broadcasted_iota(jnp.int32, (YS, XS), 1)


def signed_sum(vector, parts):
    total = None
    for sign, part in zip(vector, parts):
        if sign == 0:
            continue
        if total is None:
            total = part if sign > 0 else -part
        else:
            total = total + part if sign > 0 else total - part
    return total


def momentum(get):
    parts = [None, None, None]
    for plus, minus in PAIRS:
        diff = get(plus) - get(minus)
        for axis in range(3):
            sign = DIRS[plus][axis]
            if sign:
                if parts[axis] is None:
                    parts[axis] = diff if sign > 0 else -diff
                else:
                    parts[axis] = parts[axis] + diff if sign > 0 else parts[axis] - diff
    return parts


def damping(kind, porosity):
    return jnp.where(kind == 2.0, 0.0, 1.0 - porosity)


def damped_of(moment, kind, scale):
    inlet = kind == 3.0
    return [
        scale * part + jnp.where(inlet, level, 0.0) if level else scale * part
        for part, level in zip(moment, INFLOW)
    ]


def post_collision(get, put, density, moment, kind, porosity, masked, wanted=range(19)):
    damped = damped_of(moment, kind, damping(kind, porosity))
    target = jnp.where(kind == 4.0, 1.0, density)
    square = damped[0] * damped[0] + damped[1] * damped[1] + damped[2] * damped[2]
    base = RELAX * (target - 1.5 * square)
    keep = 1.0 - RELAX
    if masked:
        inside = kind > 0.5
        base = jnp.where(inside, base, 0.0)
        damped = [jnp.where(inside, part, 0.0) for part in damped]
        keep = jnp.where(inside, keep, 0.0)
    if 0 in wanted:
        put(0, keep * get(0) + WEIGHTS[0] * base)
    for plus, minus in PAIRS:
        if plus not in wanted and minus not in wanted:
            continue
        weight = WEIGHTS[plus]
        along = signed_sum(DIRS[plus], damped)
        even = weight * base + (4.5 * RELAX * weight) * (along * along)
        odd = (3.0 * RELAX * weight) * along
        if plus in wanted:
            put(plus, keep * get(plus) + (even + odd))
        if minus in wanted:
            put(minus, keep * get(minus) + (even - odd))


def adjoint_collision(get, put, moment, kind, porosity, masked, wanted=range(19)):
    scale = damping(kind, porosity)
    damped = damped_of(moment, kind, scale)
    total = WEIGHTS[0] * get(0)
    slope = [None, None, None]
    for group in (PAIRS[:3], PAIRS[3:]):
        weight = WEIGHTS[group[0][0]]
        even_sum = None
        local = [None, None, None]
        for plus, minus in group:
            first, second = get(plus), get(minus)
            even, odd = first + second, first - second
            even_sum = even if even_sum is None else even_sum + even
            along = signed_sum(DIRS[plus], damped)
            term = odd + 3.0 * (along * even)
            for axis in range(3):
                sign = DIRS[plus][axis]
                if sign:
                    if local[axis] is None:
                        local[axis] = term if sign > 0 else -term
                    else:
                        local[axis] = local[axis] + term if sign > 0 else local[axis] - term
        total = total + weight * even_sum
        slope = [
            weight * new if old is None else old + weight * new for old, new in zip(slope, local)
        ]
    slope = [(3.0 * RELAX) * (part - total * drift) for part, drift in zip(slope, damped)]
    dot = slope[0] * moment[0] + slope[1] * moment[1] + slope[2] * moment[2]
    share = jnp.where(kind == 2.0, 0.0, -dot)
    even = jnp.where(kind == 4.0, 0.0, RELAX * total)
    back = [scale * part for part in slope]
    keep = 1.0 - RELAX
    if masked:
        inside = kind > 0.5
        even = jnp.where(inside, even, 0.0)
        back = [jnp.where(inside, part, 0.0) for part in back]
        keep = jnp.where(inside, keep, 0.0)
    if 0 in wanted:
        put(0, keep * get(0) + even)
    for plus, minus in PAIRS:
        if plus not in wanted and minus not in wanted:
            continue
        along = signed_sum(DIRS[plus], back)
        if plus in wanted:
            put(plus, keep * get(plus) + (even + along))
        if minus in wanted:
            put(minus, keep * get(minus) + (even - along))
    return share


def parity(axis):
    return lax.axis_index(axis) % 2 == 1


def edges_kernel(f_hbm, por_hbm, kind_hbm, wgt_hbm, state_ref, edge_ref, f_ref, por_ref, kind_ref, wgt_ref, sems):
    copies = [
        pltpu.make_async_copy(source, target, sems.at[at])
        for at, (source, target) in enumerate(
            ((f_hbm, f_ref), (por_hbm, por_ref), (kind_hbm, kind_ref), (wgt_hbm, wgt_ref))
        )
    ]
    for copy in copies:
        copy.start()
    for copy in copies:
        copy.wait()
    for z in range(ZS):
        get = lambda i: f_ref[i, z]
        density = functools.reduce(lambda a, b: a + b, [get(i) for i in range(19)])
        kind = kind_ref[z].astype(jnp.float32) + 1.0

        def put(i, value):
            state_ref[i, z] = value

        post_collision(get, put, density, momentum(get), kind, por_ref[z], False)
        state_ref[POR, z] = por_ref[z]
        state_ref[KIND, z] = kind
        state_ref[WGT, z] = wgt_ref[z]
    slot_of = lanes() // (2 * HALO)
    for tile in range(EDGE_TILES):
        packed = jnp.zeros((YS, XS), jnp.float32)
        for slot in range(SLOTS):
            field, z = divmod(tile * SLOTS + slot, ZS)
            if field < FIELDS:
                moved = rot(state_ref[field, z], 2 * HALO * slot + HALO, 1)
                packed = jnp.where(slot_of == slot, moved, packed)
        edge_ref[tile] = packed


def rows_kernel(state_ref, odd_ref, even_ref, edge_ref, to_odd_ref, to_even_ref):
    from_left = (lanes() % (2 * HALO) < HALO).astype(jnp.int32)
    mine = (lax.axis_index("gx") % 2).astype(jnp.int32)
    for tile in range(EDGE_TILES):
        edge_ref[tile] = jnp.where(from_left == mine, even_ref[tile], odd_ref[tile])

    def pack(plan, start, ref):
        at = 0
        for field, z, row, rows in plan:
            ref[at : at + rows] = state_ref[field, z, row : row + rows]
            at += rows
        for tile in range(EDGE_TILES):
            at = ROWS_MAIN + HALO * tile
            ref[at : at + HALO] = edge_ref[tile, start : start + HALO]

    odd = parity("gy")

    @pl.when(odd)
    def _():
        pack(ROWS_LOW, 0, to_even_ref)
        pack(ROWS_HIGH, HALO, to_odd_ref)

    @pl.when(jnp.logical_not(odd))
    def _():
        pack(ROWS_HIGH, HALO, to_even_ref)
        pack(ROWS_LOW, 0, to_odd_ref)


def planes_kernel(state_ref, edge_ref, odd_ref, even_ref, wide_ref, side_ref, to_odd_ref, to_even_ref):
    for field in range(FIELDS):
        for z in range(ZS):
            wide_ref[field, z, 0] = state_ref[field, z]
    for tile in range(EDGE_TILES):
        side_ref[tile, 0] = edge_ref[tile]

    def unpack(plan, start, ref):
        at = 0
        for field, z, row, rows in plan:
            wide_ref[field, z, 1, row : row + rows] = ref[at : at + rows]
            at += rows
        for tile in range(EDGE_TILES):
            at = ROWS_MAIN + HALO * tile
            side_ref[tile, 1, start : start + HALO] = ref[at : at + HALO]

    odd = parity("gy")

    @pl.when(odd)
    def _():
        unpack(ROWS_HIGH, HALO, even_ref)
        unpack(ROWS_LOW, 0, odd_ref)

    @pl.when(jnp.logical_not(odd))
    def _():
        unpack(ROWS_LOW, 0, even_ref)
        unpack(ROWS_HIGH, HALO, odd_ref)

    def pack(plan, ref):
        for at, (field, z) in enumerate(plan):
            ref[at] = wide_ref[field, z]
        for tile in range(EDGE_TILES):
            ref[len(plan) + tile] = side_ref[tile]

    odd_z = parity("gz")

    @pl.when(odd_z)
    def _():
        pack(DOWN, to_even_ref)
        pack(UP, to_odd_ref)

    @pl.when(jnp.logical_not(odd_z))
    def _():
        pack(UP, to_even_ref)
        pack(DOWN, to_odd_ref)


def join(main, packed, slot):
    main = main.reshape(2 * YS, XS)
    side = rot(packed.reshape(2 * YS, XS), XS - HALO - 2 * HALO * slot, 1)
    return jnp.concatenate([main, side], axis=1)


def forward_kernel(scale, wide_ref, side_ref, odd_ref, even_ref, aux_ref, flow_ref, part_ref, f_ref):
    odd = parity("gz")

    def field_at(field, z):
        own = z % ZS
        tile, slot = divmod(field * ZS + own, SLOTS)
        if 0 <= z < ZS:
            return join(wide_ref[field, z], side_ref[tile], slot)
        plan = UP if z < 0 else DOWN
        main, side = plan.index((field, own)), len(plan) + tile
        first, second = (even_ref, odd_ref) if z < 0 else (odd_ref, even_ref)
        return join(
            jnp.where(odd, first[main], second[main]),
            jnp.where(odd, first[side], second[side]),
            slot,
        )

    for z in range(-1, ZS + 1):
        at = z + 1
        density = None
        moment = [None, None, None]
        for c in range(19):
            cx, cy, cz = DIRS[c]
            value = rot(rot(field_at(c, z - cz), cy, 0), cx, 1)
            f_ref[c, at] = value
            density = value if density is None else density + value
        get = lambda i: f_ref[i, at]
        moment = momentum(get)
        porosity, kind = field_at(POR, z), field_at(KIND, z)
        for axis in range(3):
            aux_ref[axis, at] = moment[axis]
        aux_ref[3, at] = porosity
        aux_ref[4, at] = kind

        def put(i, value):
            f_ref[i, at] = value

        wanted = [i for i in range(1, 19) if 0 <= z + DIRS[i][2] < ZS]
        post_collision(get, put, density, moment, kind, porosity, True, wanted)

    partial = jnp.zeros((YS, XS), jnp.float32)
    slot_of = lax.broadcasted_iota(jnp.int32, (2 * YS, XS), 1) // (2 * HALO)
    packed = jnp.zeros((2 * YS, XS), jnp.float32)
    for z in range(ZS):
        def arrived(i):
            cx, cy, cz = DIRS[i]
            return rot(rot(f_ref[i, z - cz + 1], cy, 0), cx, 1)

        moment = momentum(arrived)
        weight = field_at(WGT, z)
        for axis in range(3):
            flow = weight * moment[axis]
            partial = partial + flow[:YS, :XS] * moment[axis][:YS, :XS]
            slot = axis * ZS + z
            flow_ref[slot] = flow[:, :XS].reshape(2, YS, XS)
            moved = rot(flow[:, XS:], 2 * HALO * slot + HALO, 1)
            packed = jnp.where(slot_of == slot, moved, packed)
    flow_ref[3 * ZS] = packed.reshape(2, YS, XS)
    total = scale * jnp.sum(partial, axis=0, keepdims=True)
    part_ref[...] = jnp.broadcast_to(total[None], part_ref.shape)


def backward_kernel(
    flow_ref, even_ref, odd_ref, aux_ref, f_ref, por_ref, kind_ref, adjoint_ref, share_ref, g_ref
):
    odd = parity("gz")

    def flow_at(axis, z):
        slot = axis * ZS + z % ZS
        if 0 <= z < ZS:
            return join(flow_ref[slot], flow_ref[3 * ZS], slot)
        first, second = (even_ref, odd_ref) if z < 0 else (odd_ref, even_ref)
        return join(
            jnp.where(odd, first[slot], second[slot]),
            jnp.where(odd, first[3 * ZS], second[3 * ZS]),
            slot,
        )

    flows = [[flow_at(axis, z) for axis in range(3)] for z in range(-2, ZS + 2)]
    shares = []
    for z in range(-1, ZS + 1):
        at = z + 1
        g_ref[0, at] = jnp.zeros((2 * YS, 2 * XS), jnp.float32)
        for i in range(1, 19):
            cx, cy, cz = DIRS[i]
            seed = signed_sum(DIRS[i], flows[z + cz + 2])
            g_ref[i, at] = rot(rot(seed, -cy, 0), -cx, 1)
        get = lambda i: g_ref[i, at]

        def put(i, value):
            g_ref[i, at] = value

        moment = [aux_ref[axis, at] for axis in range(3)]
        wanted = [i for i in range(19) if 0 <= z - DIRS[i][2] < ZS]
        share = adjoint_collision(get, put, moment, aux_ref[4, at], aux_ref[3, at], True, wanted)
        if 0 <= z < ZS:
            shares.append(share[:YS, :XS])
    for z in range(ZS):
        for i in range(19):
            cx, cy, cz = DIRS[i]
            value = rot(g_ref[i, z + cz + 1], -cy, 0)[:YS]
            adjoint_ref[i, z] = rot(value, -cx, 1)[:, :XS]
        carried = lambda i: adjoint_ref[i, z]

        def put_out(i, value):
            adjoint_ref[i, z] = value

        moment = momentum(lambda i: f_ref[i, z])
        kind = kind_ref[z].astype(jnp.float32) + 1.0
        share = adjoint_collision(carried, put_out, moment, kind, por_ref[z], False)
        share_ref[z] = shares[z] + share


def spread_kernel(in_ref, out_ref):
    out_ref[...] = jnp.broadcast_to(jnp.sum(in_ref[...], axis=0, keepdims=True), out_ref.shape)


def call(kernel, outs, scratch=(), **options):
    shapes = tuple(jax.ShapeDtypeStruct(shape, jnp.float32) for shape in outs)
    return pl.pallas_call(
        kernel,
        out_shape=shapes if len(shapes) > 1 else shapes[0],
        scratch_shapes=[
            pltpu.VMEM(shape, jnp.float32) if isinstance(shape, tuple) else shape for shape in scratch
        ],
        compiler_params=pltpu.CompilerParams(vmem_limit_bytes=VMEM_LIMIT),
        **options,
    )


def swap(axis, to_even, to_odd, even_first=False):
    count = lax.axis_size(axis)

    def partners(first):
        return [
            pair for low in range(first, count - 1, 2) for pair in ((low, low + 1), (low + 1, low))
        ]

    if even_first:
        even = lax.ppermute(to_even, axis, partners(0))
        odd = lax.ppermute(to_odd, axis, partners(1))
    else:
        odd = lax.ppermute(to_odd, axis, partners(1))
        even = lax.ppermute(to_even, axis, partners(0))
    return odd, even


def columns():
    sizes = [lax.axis_size(axis) for axis in ("gx", "gy", "gz")]
    places = [(x, y) for x in range(sizes[0]) for y in range(sizes[1])]
    places.sort(key=lambda place: (place[1] // 4 * sizes[0] + place[0], place[1] % 4), reverse=True)
    turn = len(places) // 8
    places = places[turn:] + places[:turn]
    return [[(x * sizes[1] + y) * sizes[2] + z for x, y in places] for z in range(sizes[2])]


def per_device(checkpoint, porosity, cell_kind, objective_weight):
    brick = (ZS, YS, XS)
    state, edge = call(
        edges_kernel,
        [(FIELDS,) + brick, (EDGE_TILES, YS, XS)],
        [(19,) + brick, brick, pltpu.VMEM(brick, jnp.int32), brick, pltpu.SemaphoreType.DMA((4,))],
        in_specs=[pl.BlockSpec(memory_space=pl.ANY)] * 4,
    )(
        *(
            pltpu.with_memory_space_constraint(value, pltpu.HBM)
            for value in (checkpoint, porosity, cell_kind, objective_weight)
        )
    )
    rows = (ROWS_MSG, XS)
    edge, to_odd, to_even = call(rows_kernel, [(EDGE_TILES, YS, XS), rows, rows])(
        state, *swap("gx", edge, edge)
    )
    planes = (ZMSG, 2, YS, XS)
    wide, side, to_odd, to_even = call(
        planes_kernel, [(FIELDS, ZS, 2, YS, XS), (EDGE_TILES, 2, YS, XS), planes, planes]
    )(state, edge, *swap("gy", to_even, to_odd))
    field = (ZS + 2, 2 * YS, 2 * XS)
    group = lax.axis_size("gz")
    plane = lax.axis_size("gx") * lax.axis_size("gy")
    cells = group * plane * ZS * YS * XS
    aux, flow, part = call(
        functools.partial(forward_kernel, 0.5 / cells),
        [(5,) + field, (3 * ZS + 1, 2, YS, XS), (group, 1, XS)],
        [(19,) + field],
    )(wide, side, *swap("gz", to_even, to_odd))
    flow_odd, flow_even = swap("gz", flow, flow, True)
    falling = list(range(group))[::-1]
    turned = [falling[group // 8 :] + falling[: group // 8]]
    part = lax.all_to_all(part, "gz", 0, 0, axis_index_groups=turned, tiled=True)
    part = call(spread_kernel, [(plane, 1, XS)])(part)
    part = lax.all_to_all(
        part, ("gx", "gy", "gz"), 0, 0, axis_index_groups=columns(), tiled=True
    )
    objective = jnp.sum(part)
    adjoint, share = call(backward_kernel, [(19,) + brick, brick], [(19,) + field])(
        flow, flow_even, flow_odd, aux, checkpoint, porosity, cell_kind
    )
    return adjoint, share, objective


def solution(mesh):
    cells = P("gz", "gy", "gx")
    populations = P(None, "gz", "gy", "gx")
    return jax.shard_map(
        per_device,
        mesh=mesh,
        in_specs=(populations, cells, cells, cells),
        out_specs=(populations, cells, P()),
        check_vma=False,
    )
```
